32 devices in a mesh: grp: 2 (over y), loan: 4 (over z), feat: 4 (over x, core).
Axes of the slice: x: 2, y: 2, z: 4, core: 2. Of those that a mesh axis runs over, the one named last changes fastest.
Arguments:
- design: bfloat16 [16384, 4096], P(('grp', 'loan'), 'feat'), parts along dimension 0, may hold values from -6 to 6
- labels: int32 [16384], P(('grp', 'loan')), parts along dimension 0, may hold values from 0 to 1
- pool_ids: int32 [16384], P(('grp', 'loan')), parts along dimension 0, may hold values from 0 to 255, as said below
- pool_region_index: int32 [512], P(('grp', 'loan')), parts along dimension 0, may hold values from 0 to 63
- step_size: float32 [32], P('grp'), parts along dimension 0, may hold values from 0.005 to 0.02
- beta: float32 [32, 4096], P('grp', 'feat'), parts along dimension 0, may hold values from -0.09375 to 0.09375
- pools: float32 [32, 256, 256], P('grp', 'loan', 'feat'), parts along dimension 0, may hold values from -0.5 to 0.5
- regions: float32 [32, 64, 256], P('grp', None, 'feat'), parts along dimension 0, may hold values from -0.5 to 0.5
- beta_momentum: float32 [32, 4096], P('grp', 'feat'), parts along dimension 0, may hold values from -6 to 6
- pool_momentum: float32 [32, 256, 256], P('grp', 'loan', 'feat'), parts along dimension 0, may hold values from -6 to 6
- region_momentum: float32 [32, 64, 256], P('grp', None, 'feat'), parts along dimension 0, may hold values from -6 to 6
Outputs:
- beta_next: float32 [32, 4096], P('grp', 'feat'), parts along dimension 0
- pools_next: float32 [32, 256, 256], P('grp', 'loan', 'feat'), parts along dimension 0
- regions_next: float32 [32, 64, 256], P('grp', None, 'feat'), parts along dimension 0
- beta_momentum_next: float32 [32, 4096], P('grp', 'feat'), parts along dimension 0
- pool_momentum_next: float32 [32, 256, 256], P('grp', 'loan', 'feat'), parts along dimension 0
- region_momentum_next: float32 [32, 64, 256], P('grp', None, 'feat'), parts along dimension 0
The draws below stay inside these ranges and needn't reach their ends.
There are 2 independent parts, one for each index of `grp`. The reference program is written for one: setup_inputs(seed, part) draws one part's arguments, and reference() takes and returns one part's arrays. A program takes and returns all parts, laid end to end along the dimension named above; each array names one. Nothing has to cross between parts.
Inputs may be any that keep to these rules, and one draw needn't show every extreme that they name: `pool_ids`: in each aligned block of 2048 loans (block l counted from 0) the pool ids lie in l * 64 to (l + 1) * 64 - 1 and do not fall along the block.
All inputs are finite; a program needn't handle non-finite values.
Results may differ from the reference program's by a relative error of at most 0.0006.
Values may be sent and summed in bfloat16 or wider, within the bound.
No kernel may reach another device: no remote copies, remote signals or barrier semaphores. Data moves between devices by JAX's collectives and lax.ppermute only.
A program may use at most 64 MiB of HBM per device.

```python
import math
import jax
import jax.numpy as jnp
from jax import lax

F = 4096
G = 256
R = 64
CHAINS = 16
ROWS_DEV = 2048
POOLS_DEV = 64
LOANS = 8192
POOLS = 256
N_LOAN = 4


def draw_pool_ids(key, part):
    blocks = jax.random.randint(key, (N_LOAN, ROWS_DEV), 0, POOLS_DEV)
    blocks = jnp.sort(blocks, axis=1) + jnp.arange(N_LOAN, dtype=jnp.int32)[:, None] * POOLS_DEV
    return blocks.reshape(-1).astype(jnp.int32)


def plant(entries, stream_key, low, high):
    index_at = [jax.random.randint(jax.random.fold_in(stream_key, axis), (), 0, length) for axis, length in enumerate(entries.shape)]
    longest = entries.shape.index(max(entries.shape))
    beside = index_at[:longest] + [(index_at[longest] + 1) % entries.shape[longest]] + index_at[longest + 1:]
    return entries.at[tuple(index_at)].set(low).at[tuple(beside)].set(high)


def steps_of(key, shape, pieces, low, top_value):
    level, own = 1.0, jax.random.fold_in(key, 6)
    for axis_at, blocks in pieces:
        draws = jnp.exp(jax.random.uniform(jax.random.fold_in(own, axis_at), (blocks,), jnp.float32, low / len(pieces), top_value / len(pieces)))
        level = level * jnp.repeat(draws, shape[axis_at] // blocks).reshape([-1 if axis == axis_at else 1 for axis in range(len(shape))])
    return level


def noise(rng, dims, spread, bound, cuts=(), kind=jnp.bfloat16):
    factor_of = steps_of(rng, dims, cuts, -0.22, 0.18) if cuts else 1.0
    drawn = jax.random.normal(rng, dims, jnp.float32) * spread * factor_of
    return jnp.minimum(jnp.maximum(drawn, -bound), bound).astype(kind)


def setup_inputs(seed: int = 0, part: int = 0) -> dict:
    key_of = jax.random.split(jax.random.key(seed), 12)
    part_splits = jax.random.split(jax.random.fold_in(key_of[11], part), 12)
    return {
        "design": noise(part_splits[0], (LOANS, F), 1.0, 6.0, ((0, 4), (1, 4))),
        "labels": plant(jax.random.randint(part_splits[1], (LOANS,), 0, 2), jax.random.fold_in(part_splits[1], 1), 0, 1).astype(jnp.int32),
        "pool_ids": draw_pool_ids(jax.random.fold_in(jax.random.fold_in(key_of[11], part), 71), part),
        "pool_region_index": plant(jax.random.randint(part_splits[3], (POOLS,), 0, R), jax.random.fold_in(part_splits[3], 1), 0, R - 1).astype(jnp.int32),
        "step_size": jnp.clip(jnp.exp(jax.random.uniform(part_splits[4], (CHAINS,), jnp.float32, math.log(0.005), math.log(0.02))), 0.005, 0.02),
        "beta": noise(part_splits[5], (CHAINS, F), F ** -0.5, 0.09375, ((1, 4),), jnp.float32),
        "pools": noise(part_splits[6], (CHAINS, POOLS, G), 0.0625, 0.5, ((1, 4), (2, 4)), jnp.float32),
        "regions": noise(part_splits[7], (CHAINS, R, G), 0.0625, 0.5, ((2, 4),), jnp.float32),
        "beta_momentum": noise(part_splits[8], (CHAINS, F), 1.0, 6.0, ((1, 4),), jnp.float32),
        "pool_momentum": noise(part_splits[9], (CHAINS, POOLS, G), 1.0, 6.0, ((1, 4), (2, 4)), jnp.float32),
        "region_momentum": noise(part_splits[10], (CHAINS, R, G), 1.0, 6.0, ((2, 4),), jnp.float32),
    }


MATMUL_ACCURACY = 256.0


def gradient(design, labels, pool_ids, pool_region_index, b, upper_operand, lower_operand):
    stride = F // G
    slope_feats = design[:, ::stride].astype(jnp.float32)
    b16 = b.astype(jnp.bfloat16)
    linear = lax.dot_general(b16, design, (((1,), (1,)), ((), ())), preferred_element_type=jnp.float32)
    term = lax.map(lambda uc: jnp.sum(slope_feats * uc[pool_ids], axis=1), upper_operand)
    logit = linear + term
    resid = (labels.astype(jnp.float32)[None, :] - jax.nn.sigmoid(logit)).astype(jnp.bfloat16)
    xt = lax.dot_general(resid, design, (((1,), (0,)), ((), ())), preferred_element_type=jnp.float32)
    gb = xt - F * b
    rf = resid.astype(jnp.float32)
    lik = lax.map(lambda rc: jax.ops.segment_sum(slope_feats * rc[:, None], pool_ids, num_segments=POOLS), rf)
    selected_operand = lower_operand[:, pool_region_index, :]
    device_index = MATMUL_ACCURACY * (upper_operand - selected_operand)
    gu = lik - device_index
    sums = jax.ops.segment_sum(jnp.moveaxis(device_index, 1, 0), pool_region_index, num_segments=R)
    gv = jnp.moveaxis(sums, 0, 1) - MATMUL_ACCURACY * lower_operand
    return gb, gu, gv


def reference(design, labels, pool_ids, pool_region_index, step_size, beta, pools, regions, beta_momentum, pool_momentum, region_momentum):
    half = 0.5 * step_size
    h2 = half[:, None]
    h3 = half[:, None, None]
    e2 = step_size[:, None]
    e3 = step_size[:, None, None]
    gb, gu, gv = gradient(design, labels, pool_ids, pool_region_index, beta, pools, regions)
    mb = beta_momentum + h2 * gb
    mu = pool_momentum + h3 * gu
    mv = region_momentum + h3 * gv
    beta_next = beta + e2 * mb
    pools_next = pools + e3 * mu
    regions_next = regions + e3 * mv
    gb, gu, gv = gradient(design, labels, pool_ids, pool_region_index, beta_next, pools_next, regions_next)
    return beta_next, pools_next, regions_next, mb + h2 * gb, mu + h3 * gu, mv + h3 * gv
```

```python
import jax
import jax.numpy as jnp
from jax import lax
from jax.experimental import pallas as pl
from jax.experimental.pallas import tpu as pltpu
from jax.sharding import PartitionSpec as P

PREC = 256.0
SCALE = 1.0 / 16.0
TILE = 256
VMEM_LIMIT = 24 * 1024 * 1024
NT = (((1,), (1,)), ((), ()))
NN = (((1,), (0,)), ((), ()))
F32 = jnp.float32
BF16 = jnp.bfloat16


def whole():
    return pl.BlockSpec(memory_space=pltpu.VMEM)


def params():
    return pltpu.CompilerParams(vmem_limit_bytes=VMEM_LIMIT)


def split_table(u):
    flat = u.reshape(u.shape[0] * u.shape[1], u.shape[2])
    high = flat.astype(BF16)
    low = (flat - high.astype(F32)).astype(BF16)
    return jnp.concatenate([high, low], axis=1)


def slope_term(table_ref, slopes, ids, chains, owned):
    tile = slopes.shape[1]
    stacked = jnp.concatenate([slopes, slopes], axis=0)
    sub = lax.broadcasted_iota(jnp.int32, (8, tile), 0)
    masks = [(sub + 8 * q) == ids for q in range(owned // 8)]
    rows = []
    few = 4
    for c in range(0, chains, few):
        part = lax.dot_general(
            table_ref[c * owned : (c + few) * owned, :], stacked, NN, preferred_element_type=F32
        ).reshape(few, owned, tile)
        for k in range(few):
            acc = jnp.zeros((8, tile), F32)
            for q in range(owned // 8):
                acc = jnp.where(masks[q], part[k, 8 * q : 8 * q + 8, :], acc)
            rows.append(jnp.sum(acc, axis=0, keepdims=True))
    return jnp.concatenate(rows, axis=0)


def in_hbm(x):
    return pltpu.with_memory_space_constraint(x, pltpu.HBM)


def tile_copies(source, target, sems):
    copies = []
    for t in range(source.shape[0] // TILE):
        rows = pl.ds(t * TILE, TILE)
        copies.append(pltpu.make_async_copy(source.at[rows], target.at[rows], sems.at[t]))
    for copy in copies:
        copy.start()
    return copies


def design_scratch(design):
    rows, feats = design.shape
    return [pltpu.VMEM((rows, feats), BF16), pltpu.SemaphoreType.DMA((rows // TILE,))]


def first_logits(design, ids, beta, pools, stride):
    rows, feats = design.shape
    chains, owned, slopes = pools.shape

    def kernel(design_hbm, ids_ref, beta_hbm, pools_hbm, slope_ref, part_ref, w, table, b_ref, u_ref, sem, kept, sems):
        small = [
            pltpu.make_async_copy(pools_hbm, u_ref, sem.at[0]),
            pltpu.make_async_copy(beta_hbm, b_ref, sem.at[1]),
        ]
        for copy in small:
            copy.start()
        copies = tile_copies(design_hbm, kept, sems)
        g = lax.broadcasted_iota(jnp.int32, (slopes, feats), 0)
        f = lax.broadcasted_iota(jnp.int32, (slopes, feats), 1)
        w[:slopes, :] = jnp.where(f == g * stride, 1.0, 0.0).astype(BF16)
        small[0].wait()
        table[...] = split_table(u_ref[...])
        small[1].wait()
        w[slopes:, :] = b_ref[...].astype(BF16)
        first = lax.axis_index("loan") * owned
        for t, copy in enumerate(copies):
            copy.wait()
            cols = slice(t * TILE, (t + 1) * TILE)
            both = lax.dot_general(w[...], kept[cols, :], NT, preferred_element_type=F32)
            slope = both[:slopes, :].astype(BF16)
            slope_ref[:, cols] = slope
            term = slope_term(table, slope, ids_ref[:, cols] - first, chains, owned)
            part_ref[:, cols] = (both[slopes:, :] + term) * SCALE

    return pl.pallas_call(
        kernel,
        in_specs=[pl.BlockSpec(memory_space=pl.ANY), whole()] + [pl.BlockSpec(memory_space=pl.ANY)] * 2,
        out_specs=[whole(), whole()],
        out_shape=[
            jax.ShapeDtypeStruct((slopes, rows), BF16),
            jax.ShapeDtypeStruct((chains, rows), F32),
        ],
        scratch_shapes=[
            pltpu.VMEM((slopes + chains, feats), BF16),
            pltpu.VMEM((chains * owned, 2 * slopes), BF16),
            pltpu.VMEM(beta.shape, F32),
            pltpu.VMEM(pools.shape, F32),
            pltpu.SemaphoreType.DMA((2,)),
        ]
        + design_scratch(design),
        compiler_params=params(),
        name="first_logits",
    )(in_hbm(design), ids, in_hbm(beta), in_hbm(pools))


def population_gradient(resid, design):
    def kernel(resid_ref, design_hbm, out_ref, kept, sems):
        total = None
        for t, copy in enumerate(tile_copies(design_hbm, kept, sems)):
            copy.wait()
            cols = slice(t * TILE, (t + 1) * TILE)
            part = lax.dot_general(
                resid_ref[:, cols], kept[cols, :], NN, preferred_element_type=F32
            )
            total = part if total is None else total + part
        out_ref[...] = SCALE * total

    return pl.pallas_call(
        kernel,
        in_specs=[whole(), pl.BlockSpec(memory_space=pl.ANY)],
        out_specs=whole(),
        out_shape=jax.ShapeDtypeStruct((resid.shape[0], design.shape[1]), F32),
        scratch_shapes=design_scratch(design),
        compiler_params=params(),
        name="population_gradient",
    )(resid, in_hbm(design))


def pool_sums(resid_ref, slope_ref, ids_ref, chains, owned):
    rows = resid_ref.shape[1]
    total = None
    sub = lax.broadcasted_iota(jnp.int32, (owned, TILE), 0)
    for t in range(rows // TILE):
        cols = slice(t * TILE, (t + 1) * TILE)
        mask = sub == ids_ref[:, cols] - lax.axis_index("loan") * owned
        resid = resid_ref[:, cols].astype(F32)
        table = jnp.concatenate(
            [jnp.where(mask, resid[c : c + 1, :], 0.0).astype(BF16) for c in range(chains)], axis=0
        )
        part = lax.dot_general(table, slope_ref[:, cols], NT, preferred_element_type=F32)
        total = part if total is None else total + part
    return total.reshape(chains, owned, slope_ref.shape[0])


def pool_step(resid, slope, ids, base, scale_pos, scale_mom, mom_base):
    chains, owned, slopes = base.shape
    rows = resid.shape[1]

    def kernel(resid_ref, slope_ref, ids_ref, base_ref, sp_ref, sm_ref, mb_ref, next_ref, half_ref, term_ref, table):
        lik = pool_sums(resid_ref, slope_ref, ids_ref, chains, owned)
        half = mb_ref[...] + sm_ref[...] * lik
        half_ref[...] = half
        ahead = base_ref[...] + sp_ref[...] * half
        next_ref[...] = ahead
        table[...] = split_table(ahead)
        for t in range(rows // TILE):
            cols = slice(t * TILE, (t + 1) * TILE)
            term_ref[:, cols] = slope_term(
                table,
                slope_ref[:, cols],
                ids_ref[:, cols] - lax.axis_index("loan") * owned,
                chains,
                owned,
            )

    return pl.pallas_call(
        kernel,
        in_specs=[whole()] * 7,
        out_specs=[whole()] * 3,
        out_shape=[
            jax.ShapeDtypeStruct(base.shape, F32),
            jax.ShapeDtypeStruct(base.shape, F32),
            jax.ShapeDtypeStruct((chains, rows), F32),
        ],
        scratch_shapes=[pltpu.VMEM((chains * owned, 2 * slopes), BF16)],
        compiler_params=params(),
        name="pool_step",
    )(resid, slope, ids, base, scale_pos, scale_mom, mom_base)


def pool_likelihood(resid, slope, ids, chains, owned):
    def kernel(resid_ref, slope_ref, ids_ref, out_ref):
        out_ref[...] = pool_sums(resid_ref, slope_ref, ids_ref, chains, owned)

    return pl.pallas_call(
        kernel,
        in_specs=[whole()] * 3,
        out_specs=whole(),
        out_shape=jax.ShapeDtypeStruct((chains, owned, slope.shape[0]), F32),
        compiler_params=params(),
        name="pool_likelihood",
    )(resid, slope, ids)


def next_logits(design, coef, term):
    def kernel(design_hbm, coef_ref, term_ref, out_ref, kept, sems):
        coef16 = coef_ref[...].astype(BF16)
        for t, copy in enumerate(tile_copies(design_hbm, kept, sems)):
            copy.wait()
            cols = slice(t * TILE, (t + 1) * TILE)
            linear = lax.dot_general(coef16, kept[cols, :], NT, preferred_element_type=F32)
            out_ref[:, cols] = SCALE * (term_ref[:, cols] + linear)

    return pl.pallas_call(
        kernel,
        in_specs=[pl.BlockSpec(memory_space=pl.ANY), whole(), whole()],
        out_specs=whole(),
        out_shape=jax.ShapeDtypeStruct(term.shape, F32),
        scratch_shapes=design_scratch(design),
        compiler_params=params(),
        name="next_logits",
    )(in_hbm(design), coef, term)


def ahead_by(k, size, stride, group):
    perm = []
    for i in range(size):
        digit = (i // stride) % group
        perm.append((i, i + ((digit + k) % group - digit) * stride))
    return perm


def total_over(x, axis):
    size = lax.axis_size(axis)
    stride = 1
    while stride < size:
        group = min(4, size // stride)
        own = lax.optimization_barrier(x.astype(jnp.float16))
        parts = [own] + [
            lax.ppermute(own, axis, ahead_by(k, size, stride, group)) for k in range(1, group)
        ]
        parts = [p.astype(F32) for p in parts]
        x = parts[0] + parts[1] if group == 2 else (parts[0] + parts[2]) + (parts[1] + parts[3])
        stride *= group
    return x


def shared_sum(x, axis):
    size = lax.axis_size(axis)
    me = lax.axis_index(axis)
    width = x.shape[1] // size
    x = lax.optimization_barrier(x.astype(jnp.float16))

    def block(k):
        return lax.dynamic_slice_in_dim(x, lax.rem(me + k, size) * width, width, 1)

    mine = block(0).astype(F32)
    for k in range(1, size):
        mine = mine + lax.ppermute(block(k), axis, ahead_by(k, size, 1, size)).astype(F32)
    mine = lax.optimization_barrier(mine.astype(jnp.float16))
    found = [mine] + [lax.ppermute(mine, axis, ahead_by(k, size, 1, size)) for k in range(1, size)]
    back = jnp.concatenate(found[::-1], axis=1)
    return jnp.roll(back, (me + 1) * width, axis=1).astype(F32)


def couple(x):
    return jnp.concatenate(jnp.split(x, 2, axis=0), axis=2)


def uncouple(x):
    return jnp.concatenate(jnp.split(x, 2, axis=2), axis=0)


def residual(part, labels):
    logit = total_over(part, "feat") * (1.0 / SCALE)
    return (labels.astype(F32)[None, :] - jax.nn.sigmoid(logit)).astype(BF16)


def body(
    design,
    labels,
    pool_ids,
    pool_region_index,
    step_size,
    beta,
    pools,
    regions,
    beta_momentum,
    pool_momentum,
    region_momentum,
):
    rows, feats = design.shape
    chains, owned, slopes = pools.shape
    n_regions = regions.shape[1]
    total_feats = float(feats * lax.axis_size("feat"))
    half = 0.5 * step_size
    h2, h3 = half[:, None], half[:, None, None]
    e2, e3 = step_size[:, None], step_size[:, None, None]
    ids = pool_ids[None, :]

    slope, part = first_logits(design, ids, beta, pools, feats // slopes)

    lookup = (
        pool_region_index[:, None] == jnp.arange(n_regions, dtype=jnp.int32)[None, :]
    ).astype(F32)
    chosen = jnp.einsum("pr,crg->cpg", lookup, regions, precision=lax.Precision.HIGHEST)
    dev = PREC * (pools - chosen)
    counts = jnp.sum(lookup, axis=0)[None, :, None]
    region_dev = jnp.einsum("pr,cpg->crg", lookup, dev, precision=lax.Precision.HIGHEST)
    counts = jnp.broadcast_to(counts, (1, n_regions, 2 * slopes))
    mom_base = pool_momentum - h3 * dev

    resid = residual(part, labels)
    gb = population_gradient(resid, design)
    resid, gb = lax.optimization_barrier((resid, gb))
    pools_next, pool_half, term = pool_step(
        resid,
        slope,
        ids,
        pools,
        jnp.broadcast_to(e3, (chains, 1, slopes)),
        jnp.broadcast_to(h3, (chains, 1, slopes)),
        mom_base,
    )
    gb = total_over(gb, "loan") * (1.0 / SCALE) - total_feats * beta
    beta_half = beta_momentum + h2 * gb
    beta_next = beta + e2 * beta_half

    part = next_logits(design, beta_next, term)
    moved = jnp.einsum("pr,cpg->crg", lookup, e3 * pool_half, precision=lax.Precision.HIGHEST)
    shared = jnp.concatenate([couple(region_dev), couple(moved), counts], axis=0)
    shared = shared_sum(SCALE * shared, "loan") * (1.0 / SCALE)
    pairs = chains // 2
    region_dev, moved = uncouple(shared[:pairs]), uncouple(shared[pairs : 2 * pairs])
    counts = shared[2 * pairs :, :, :slopes]
    region_half = region_momentum + h3 * (region_dev - PREC * regions)
    regions_next = regions + e3 * region_half

    resid = residual(part, labels)
    gb = population_gradient(resid, design)
    resid, gb = lax.optimization_barrier((resid, gb))
    lik = pool_likelihood(resid, slope, ids, chains, owned)
    gb = total_over(gb, "loan") * (1.0 / SCALE) - total_feats * beta_next
    beta_out = beta_half + h2 * gb

    chosen = jnp.einsum("pr,crg->cpg", lookup, regions_next, precision=lax.Precision.HIGHEST)
    pool_out = pool_half + h3 * (lik - PREC * (pools_next - chosen))
    gv = region_dev + PREC * (moved - counts * (regions_next - regions)) - PREC * regions_next
    region_out = region_half + h3 * gv
    return (beta_next, pools_next, regions_next, beta_out, pool_out, region_out)


def solution(mesh):
    in_specs = (
        P(("grp", "loan"), "feat"),
        P(("grp", "loan")),
        P(("grp", "loan")),
        P(("grp", "loan")),
        P("grp"),
        P("grp", "feat"),
        P("grp", "loan", "feat"),
        P("grp", None, "feat"),
        P("grp", "feat"),
        P("grp", "loan", "feat"),
        P("grp", None, "feat"),
    )
    out_specs = (
        P("grp", "feat"),
        P("grp", "loan", "feat"),
        P("grp", None, "feat"),
        P("grp", "feat"),
        P("grp", "loan", "feat"),
        P("grp", None, "feat"),
    )
    return jax.shard_map(body, mesh=mesh, in_specs=in_specs, out_specs=out_specs, check_vma=False)
```

```python
import jax
import jax.numpy as jnp
from jax import lax
from jax.experimental import pallas as pl
from jax.experimental.pallas import tpu as pltpu
from jax.sharding import PartitionSpec as P

PREC = 256.0
SCALE = 1.0 / 16.0
TILE = 256
OCTET = 8
SPAN = 3
VMEM_LIMIT = 24 * 1024 * 1024
NT = (((1,), (1,)), ((), ()))
NN = (((1,), (0,)), ((), ()))
F32 = jnp.float32
BF16 = jnp.bfloat16


def whole():
    return pl.BlockSpec(memory_space=pltpu.VMEM)


def params():
    return pltpu.CompilerParams(vmem_limit_bytes=VMEM_LIMIT)


def fill_table(table_ref, u):
    chains, octets = len(u), u[0].shape[0] // OCTET
    for q in range(octets):
        rows = jnp.concatenate([x[q * OCTET : (q + 1) * OCTET, :] for x in u], axis=0)
        high = rows.astype(BF16)
        low = (rows - high.astype(F32)).astype(BF16)
        table_ref[q * chains * OCTET : (q + 1) * chains * OCTET, :] = jnp.concatenate([high, low], axis=1)


def window_of(ids, octets, span):
    start = jnp.clip(jnp.min(ids) // OCTET, 0, octets - span)
    return start, ids - start * OCTET


def octet_masks(ids, span):
    sub = lax.broadcasted_iota(jnp.int32, (OCTET, ids.shape[1]), 0)
    return [sub + OCTET * k == ids for k in range(span)]


def term_of_window(table_ref, slopes, ids, start, chains, span):
    tile = slopes.shape[1]
    block = chains * OCTET
    rows = pl.ds(pl.multiple_of(start * block, block), span * block)
    stacked = jnp.concatenate([slopes, slopes], axis=0)
    part = lax.dot_general(table_ref[rows, :], stacked, NN, preferred_element_type=F32)
    part = part.reshape(span, chains, OCTET, tile)
    picked = jnp.zeros((chains, OCTET, tile), F32)
    for k, mask in enumerate(octet_masks(ids, span)):
        picked = jnp.where(mask[None], part[k], picked)
    return jnp.sum(picked, axis=1)


def sums_of_window(total_ref, resid, slopes, ids, start, chains, span):
    tile = slopes.shape[1]
    block = chains * OCTET
    rows = pl.ds(pl.multiple_of(start * block, block), span * block)
    spread = jnp.broadcast_to(resid.astype(F32)[:, None, :], (chains, OCTET, tile))
    table = [jnp.where(mask[None], spread, 0.0).reshape(block, tile) for mask in octet_masks(ids, span)]
    table = jnp.concatenate(table, axis=0).astype(BF16)
    total_ref[rows, :] += lax.dot_general(table, slopes, NT, preferred_element_type=F32)


def each_tile(ids_ref, owned, visit, rest):
    octets = owned // OCTET
    span = min(SPAN, octets)
    first = lax.axis_index("loan") * owned
    tiles = ids_ref.shape[1] // TILE
    most = None
    for t in range(tiles):
        ids = ids_ref[:, t * TILE : (t + 1) * TILE] - first
        start, ids = window_of(ids, octets, span)
        visit(t, ids, start, span)
        most = ids if most is None else jnp.maximum(most, ids)

    @pl.when(jnp.max(most) >= span * OCTET)
    def _():
        @pl.loop(0, tiles)
        def _(t):
            cols = pl.ds(pl.multiple_of(t * TILE, TILE), TILE)
            ids = ids_ref[:, cols] - first
            start, _ = window_of(ids, octets, span)

            @pl.loop(start + span, jnp.max(ids) // OCTET + 1)
            def _(q):
                rest(cols, ids - q * OCTET, q)


def all_terms(table_ref, slope_ref, ids_ref, out_ref, chains, owned):
    def visit(t, ids, start, span):
        cols = slice(t * TILE, (t + 1) * TILE)
        out_ref[:, cols] = term_of_window(table_ref, slope_ref[:, cols], ids, start, chains, span)

    def rest(cols, ids, q):
        out_ref[:, cols] += term_of_window(table_ref, slope_ref[:, cols], ids, q, chains, 1)

    each_tile(ids_ref, owned, visit, rest)


def all_sums(total_ref, resid_ref, slope_ref, ids_ref, chains, owned):
    total_ref[...] = jnp.zeros(total_ref.shape, F32)

    def visit(t, ids, start, span):
        cols = slice(t * TILE, (t + 1) * TILE)
        sums_of_window(total_ref, resid_ref[:, cols], slope_ref[:, cols], ids, start, chains, span)

    def rest(cols, ids, q):
        sums_of_window(total_ref, resid_ref[:, cols], slope_ref[:, cols], ids, q, chains, 1)

    each_tile(ids_ref, owned, visit, rest)
    block = chains * OCTET
    return [
        jnp.concatenate(
            [
                total_ref[q * block + c * OCTET : q * block + (c + 1) * OCTET, :]
                for q in range(owned // OCTET)
            ],
            axis=0,
        )
        for c in range(chains)
    ]


def in_vmem(x):
    return pltpu.with_memory_space_constraint(x, pltpu.VMEM)


def in_hbm(x):
    return pltpu.with_memory_space_constraint(x, pltpu.HBM)


def tile_copies(source, target, sems):
    copies = []
    for t in range(source.shape[0] // TILE):
        rows = pl.ds(t * TILE, TILE)
        copies.append(pltpu.make_async_copy(source.at[rows], target.at[rows], sems.at[t]))
    for copy in copies:
        copy.start()
    return copies


def design_scratch(design):
    rows, feats = design.shape
    return [pltpu.VMEM((rows, feats), BF16), pltpu.SemaphoreType.DMA((rows // TILE,))]


def first_logits(design, ids, beta, pools, stride):
    rows, feats = design.shape
    chains, owned, slopes = pools.shape

    def kernel(design_ref, ids_ref, beta_hbm, pools_hbm, slope_ref, part_ref, w, table, linear, b_ref, u_ref, sem):
        small = [
            pltpu.make_async_copy(pools_hbm, u_ref, sem.at[0]),
            pltpu.make_async_copy(beta_hbm, b_ref, sem.at[1]),
        ]
        for copy in small:
            copy.start()
        g = lax.broadcasted_iota(jnp.int32, (slopes, feats), 0)
        f = lax.broadcasted_iota(jnp.int32, (slopes, feats), 1)
        w[:slopes, :] = jnp.where(f == g * stride, 1.0, 0.0).astype(BF16)
        small[0].wait()
        fill_table(table, [u_ref[c] for c in range(chains)])
        small[1].wait()
        w[slopes:, :] = b_ref[...].astype(BF16)
        for t in range(rows // TILE):
            cols = slice(t * TILE, (t + 1) * TILE)
            both = lax.dot_general(w[...], design_ref[cols, :], NT, preferred_element_type=F32)
            slope_ref[:, cols] = both[:slopes, :].astype(BF16)
            linear[:, cols] = both[slopes:, :]
        all_terms(table, slope_ref, ids_ref, part_ref, chains, owned)
        part_ref[...] = SCALE * (part_ref[...] + linear[...])

    return pl.pallas_call(
        kernel,
        in_specs=[whole(), whole()] + [pl.BlockSpec(memory_space=pl.ANY)] * 2,
        out_specs=[whole(), whole()],
        out_shape=[
            jax.ShapeDtypeStruct((slopes, rows), BF16),
            jax.ShapeDtypeStruct((chains, rows), F32),
        ],
        scratch_shapes=[
            pltpu.VMEM((slopes + chains, feats), BF16),
            pltpu.VMEM((chains * owned, 2 * slopes), BF16),
            pltpu.VMEM((chains, rows), F32),
            pltpu.VMEM(beta.shape, F32),
            pltpu.VMEM(pools.shape, F32),
            pltpu.SemaphoreType.DMA((2,)),
        ],
        compiler_params=params(),
        name="first_logits",
    )(in_vmem(design), ids, in_hbm(beta), in_hbm(pools))


def population_gradient(resid, design):
    def kernel(resid_ref, design_ref, out_ref):
        out_ref[...] = SCALE * lax.dot_general(
            resid_ref[...], design_ref[...], NN, preferred_element_type=F32
        )

    return pl.pallas_call(
        kernel,
        in_specs=[whole(), whole()],
        out_specs=whole(),
        out_shape=jax.ShapeDtypeStruct((resid.shape[0], design.shape[1]), F32),
        compiler_params=params(),
        name="population_gradient",
    )(resid, in_vmem(design))


def stacked_split(x, pieces):
    parts = []
    for _ in range(pieces):
        part = x.astype(BF16)
        parts.append(part)
        x = x - part.astype(F32)
    return jnp.concatenate(parts, axis=0)


def quad(x, j, pairs):
    return jnp.concatenate([x[k] for k in (2 * j, 2 * j + pairs, 2 * j + 1, 2 * j + 1 + pairs)], axis=1)


def region_onehot(index_ref, regions):
    shape = (regions, index_ref.shape[1])
    return jnp.where(lax.broadcasted_iota(jnp.int32, shape, 0) == index_ref[...], 1.0, 0.0)


def chosen_regions(onehot, v):
    chains, _, slopes = v.shape
    pairs = chains // 2
    table = jnp.concatenate([onehot.T.astype(BF16)] * 3, axis=1)
    found = [None] * chains
    for j in range(pairs // 2):
        got = lax.dot_general(
            table, stacked_split(quad(v, j, pairs), 3), NN, preferred_element_type=F32
        )
        for k, c in enumerate((2 * j, 2 * j + pairs, 2 * j + 1, 2 * j + 1 + pairs)):
            found[c] = got[:, k * slopes : (k + 1) * slopes]
    return found


def region_sums(onehot, x, pieces, store):
    pairs = len(x) // 2
    width = 2 * x[0].shape[1]
    table = jnp.concatenate([onehot.astype(BF16)] * pieces, axis=1)
    for j in range(pairs // 2):
        got = lax.dot_general(
            table, stacked_split(quad(x, j, pairs), pieces), NN, preferred_element_type=F32
        )
        store(2 * j, got[:, :width])
        store(2 * j + 1, got[:, width:])


def smem():
    return pl.BlockSpec(memory_space=pltpu.SMEM)


def prior(index, step, pools, regions, momentum, design):
    chains, owned, slopes = pools.shape
    n_regions = regions.shape[1]
    pairs = chains // 2

    def kernel(index_ref, step_ref, pools_ref, regions_ref, mom_ref, design_hbm, base_ref, sums_ref, kept, sem):
        copy = pltpu.make_async_copy(design_hbm, kept, sem)
        copy.start()
        onehot = region_onehot(index_ref, n_regions)
        chosen = chosen_regions(onehot, regions_ref[...])
        dev = [PREC * (pools_ref[c] - chosen[c]) for c in range(chains)]
        for c in range(chains):
            base_ref[c] = mom_ref[c] - (0.5 * step_ref[c]) * dev[c]

        def store(k, value):
            sums_ref[k] = SCALE * value

        region_sums(onehot, dev, 3, store)
        count = jnp.sum(onehot, axis=1, keepdims=True)
        sums_ref[pairs] = SCALE * jnp.broadcast_to(count, (n_regions, 2 * slopes))
        copy.wait()

    return pl.pallas_call(
        kernel,
        in_specs=[whole(), smem(), whole(), whole(), whole(), pl.BlockSpec(memory_space=pl.ANY)],
        out_specs=[whole()] * 3,
        out_shape=[
            jax.ShapeDtypeStruct(pools.shape, F32),
            jax.ShapeDtypeStruct((pairs + 1, n_regions, 2 * slopes), F32),
            pltpu.VMEM(design.shape, BF16),
        ],
        scratch_shapes=[pltpu.SemaphoreType.DMA],
        compiler_params=params(),
        name="prior",
    )(index, step, pools, regions, momentum, in_hbm(design))


def pool_step(resid, slope, ids, index, step, base, mom_base, n_regions):
    chains, owned, slopes = base.shape
    rows = resid.shape[1]
    pairs = chains // 2

    def kernel(resid_ref, slope_ref, ids_ref, index_ref, step_ref, base_ref, mb_ref, next_ref, half_ref, term_ref, sums_ref, table, total):
        lik = all_sums(total, resid_ref, slope_ref, ids_ref, chains, owned)
        way, ahead = [], []
        for c in range(chains):
            half = mb_ref[c] + (0.5 * step_ref[c]) * lik[c]
            half_ref[c] = half
            way.append(step_ref[c] * half)
            ahead.append(base_ref[c] + way[c])
            next_ref[c] = ahead[c]
        fill_table(table, ahead)
        all_terms(table, slope_ref, ids_ref, term_ref, chains, owned)

        def store(k, value):
            sums_ref[k] = SCALE * value

        region_sums(region_onehot(index_ref, n_regions), way, 2, store)

    return pl.pallas_call(
        kernel,
        in_specs=[whole()] * 4 + [smem()] + [whole()] * 2,
        out_specs=[whole()] * 4,
        out_shape=[
            jax.ShapeDtypeStruct(base.shape, F32),
            jax.ShapeDtypeStruct(base.shape, F32),
            jax.ShapeDtypeStruct((chains, rows), F32),
            jax.ShapeDtypeStruct((pairs, n_regions, 2 * slopes), F32),
        ],
        scratch_shapes=[
            pltpu.VMEM((chains * owned, 2 * slopes), BF16),
            pltpu.VMEM((chains * owned, slopes), F32),
        ],
        compiler_params=params(),
        name="pool_step",
    )(resid, slope, ids, index, step, base, mom_base)


def region_step(index, step, sums, regions, momentum, pools_next, pool_half):
    chains, owned, slopes = pools_next.shape
    n_regions = regions.shape[1]
    pairs = chains // 2

    def kernel(index_ref, step_ref, sums_ref, v_ref, m_ref, u_ref, half_ref, next_ref, mom_ref, pool_ref):
        def part(k, c):
            side = slice((c // pairs) * slopes, (c // pairs + 1) * slopes)
            return (1.0 / SCALE) * sums_ref[k + c % pairs][:, side]

        count = (1.0 / SCALE) * sums_ref[pairs][:, :slopes]
        for c in range(chains):
            v, h = v_ref[c], 0.5 * step_ref[c]
            dev = part(0, c)
            half = m_ref[c] + h * (dev - PREC * v)
            ahead = v + step_ref[c] * half
            next_ref[c] = ahead
            gain = dev + PREC * (part(pairs + 1, c) - count * (ahead - v)) - PREC * ahead
            mom_ref[c] = half + h * gain
        chosen = chosen_regions(region_onehot(index_ref, n_regions), next_ref[...])
        for c in range(chains):
            pool_ref[c] = half_ref[c] - (0.5 * step_ref[c]) * (PREC * (u_ref[c] - chosen[c]))

    return pl.pallas_call(
        kernel,
        in_specs=[whole(), smem()] + [whole()] * 5,
        out_specs=[whole()] * 3,
        out_shape=[
            jax.ShapeDtypeStruct(regions.shape, F32),
            jax.ShapeDtypeStruct(regions.shape, F32),
            jax.ShapeDtypeStruct(pools_next.shape, F32),
        ],
        compiler_params=params(),
        name="region_step",
    )(index, step, sums, regions, momentum, pools_next, pool_half)


def pool_likelihood(resid, slope, ids, step, part):
    chains, owned, slopes = part.shape

    def kernel(resid_ref, slope_ref, ids_ref, step_ref, part_ref, out_ref, total):
        lik = all_sums(total, resid_ref, slope_ref, ids_ref, chains, owned)
        for c in range(chains):
            out_ref[c] = part_ref[c] + (0.5 * step_ref[c]) * lik[c]

    return pl.pallas_call(
        kernel,
        in_specs=[whole()] * 3 + [smem(), whole()],
        out_specs=whole(),
        out_shape=jax.ShapeDtypeStruct(part.shape, F32),
        scratch_shapes=[pltpu.VMEM((chains * owned, slopes), F32)],
        compiler_params=params(),
        name="pool_likelihood",
    )(resid, slope, ids, step, part)


def next_logits(design, coef, term):
    rows = design.shape[0]

    def kernel(design_ref, coef_ref, term_ref, out_ref):
        coef16 = coef_ref[...].astype(BF16)
        for t in range(rows // TILE):
            cols = slice(t * TILE, (t + 1) * TILE)
            linear = lax.dot_general(coef16, design_ref[cols, :], NT, preferred_element_type=F32)
            out_ref[:, cols] = SCALE * (term_ref[:, cols] + linear)

    return pl.pallas_call(
        kernel,
        in_specs=[whole(), whole(), whole()],
        out_specs=whole(),
        out_shape=jax.ShapeDtypeStruct(term.shape, F32),
        compiler_params=params(),
        name="next_logits",
    )(in_vmem(design), coef, term)


def ahead_by(k, size, stride, group):
    perm = []
    for i in range(size):
        digit = (i // stride) % group
        perm.append((i, i + ((digit + k) % group - digit) * stride))
    return perm


def total_over(x, axis):
    size = lax.axis_size(axis)
    stride = 1
    while stride < size:
        group = min(4, size // stride)
        own = lax.optimization_barrier(x.astype(jnp.float16))
        parts = [own] + [
            lax.ppermute(own, axis, ahead_by(k, size, stride, group)) for k in range(1, group)
        ]
        parts = [p.astype(F32) for p in parts]
        x = parts[0] + parts[1] if group == 2 else (parts[0] + parts[2]) + (parts[1] + parts[3])
        stride *= group
    return x


def shared_sum(x, axis):
    size = lax.axis_size(axis)
    me = lax.axis_index(axis)
    width = x.shape[1] // size
    x = lax.optimization_barrier(x.astype(jnp.float16))

    def block(k):
        return lax.dynamic_slice_in_dim(x, lax.rem(me + k, size) * width, width, 1)

    mine = block(0).astype(F32)
    for k in range(1, size):
        mine = mine + lax.ppermute(block(k), axis, ahead_by(k, size, 1, size)).astype(F32)
    mine = lax.optimization_barrier(mine.astype(jnp.float16))
    found = [mine] + [lax.ppermute(mine, axis, ahead_by(k, size, 1, size)) for k in range(1, size)]
    back = jnp.concatenate(found[::-1], axis=1)
    return jnp.roll(back, (me + 1) * width, axis=1).astype(F32)


def residual(part, labels):
    logit = total_over(part, "feat") * (1.0 / SCALE)
    return (labels.astype(F32)[None, :] - jax.nn.sigmoid(logit)).astype(BF16)


def body(
    design,
    labels,
    pool_ids,
    pool_region_index,
    step_size,
    beta,
    pools,
    regions,
    beta_momentum,
    pool_momentum,
    region_momentum,
):
    rows, feats = design.shape
    chains, owned, slopes = pools.shape
    n_regions = regions.shape[1]
    total_feats = float(feats * lax.axis_size("feat"))
    half = 0.5 * step_size
    ids = pool_ids[None, :]
    index = pool_region_index[None, :]

    slope, part = first_logits(design, ids, beta, pools, feats // slopes)
    pools_at, part = lax.optimization_barrier((pools, part))
    mom_base, dev_sums, kept = prior(
        index, step_size, pools_at, regions, pool_momentum, design
    )

    resid = residual(part, labels)
    gb = population_gradient(resid, kept)
    resid, gb, mom_base, dev_sums = lax.optimization_barrier((resid, gb, mom_base, dev_sums))
    pools_next, pool_half, term, way_sums = pool_step(
        resid, slope, ids, index, step_size, pools, mom_base, n_regions
    )
    sums = shared_sum(jnp.concatenate([dev_sums, way_sums], axis=0), "loan")
    gb = total_over(gb, "loan") * (1.0 / SCALE) - total_feats * beta
    beta_half = beta_momentum + half[:, None] * gb
    beta_next = beta + step_size[:, None] * beta_half

    part = next_logits(design, beta_next, term)
    resid = residual(part, labels)
    gb = population_gradient(resid, design)
    resid, gb = lax.optimization_barrier((resid, gb))
    regions_next, region_out, pool_part = region_step(
        index, step_size, sums, regions, region_momentum, pools_next, pool_half
    )
    pool_out = pool_likelihood(resid, slope, ids, step_size, pool_part)
    gb = total_over(gb, "loan") * (1.0 / SCALE) - total_feats * beta_next
    beta_out = beta_half + half[:, None] * gb
    return (beta_next, pools_next, regions_next, beta_out, pool_out, region_out)


def solution(mesh):
    in_specs = (
        P(("grp", "loan"), "feat"),
        P(("grp", "loan")),
        P(("grp", "loan")),
        P(("grp", "loan")),
        P("grp"),
        P("grp", "feat"),
        P("grp", "loan", "feat"),
        P("grp", None, "feat"),
        P("grp", "feat"),
        P("grp", "loan", "feat"),
        P("grp", None, "feat"),
    )
    out_specs = (
        P("grp", "feat"),
        P("grp", "loan", "feat"),
        P("grp", None, "feat"),
        P("grp", "feat"),
        P("grp", "loan", "feat"),
        P("grp", None, "feat"),
    )
    return jax.shard_map(body, mesh=mesh, in_specs=in_specs, out_specs=out_specs, check_vma=False)
```

```python
import jax
import jax.numpy as jnp
from jax import lax
from jax.experimental import pallas as pl
from jax.experimental.pallas import tpu as pltpu
from jax.sharding import PartitionSpec as P

PREC = 256.0
SCALE = 1.0 / 16.0
TILE = 256
OCTET = 8
SPAN = 3
CHUNKS = 2
VMEM_LIMIT = 24 * 1024 * 1024
NT = (((1,), (1,)), ((), ()))
NN = (((1,), (0,)), ((), ()))
F32 = jnp.float32
BF16 = jnp.bfloat16


def whole():
    return pl.BlockSpec(memory_space=pltpu.VMEM)


def params():
    return pltpu.CompilerParams(vmem_limit_bytes=VMEM_LIMIT)


def fill_table(table_ref, u):
    chains, octets = len(u), u[0].shape[0] // OCTET
    for q in range(octets):
        rows = jnp.concatenate([x[q * OCTET : (q + 1) * OCTET, :] for x in u], axis=0)
        high = rows.astype(BF16)
        low = (rows - high.astype(F32)).astype(BF16)
        table_ref[q * chains * OCTET : (q + 1) * chains * OCTET, :] = jnp.concatenate([high, low], axis=1)


def window_of(ids, octets, span):
    start = jnp.clip(jnp.min(ids) // OCTET, 0, octets - span)
    return start, ids - start * OCTET


def octet_masks(ids, span):
    sub = lax.broadcasted_iota(jnp.int32, (OCTET, ids.shape[1]), 0)
    return [sub + OCTET * k == ids for k in range(span)]


def term_of_window(table_ref, slopes, ids, start, chains, span):
    tile = slopes.shape[1]
    block = chains * OCTET
    rows = pl.ds(pl.multiple_of(start * block, block), span * block)
    stacked = jnp.concatenate([slopes, slopes], axis=0)
    part = lax.dot_general(table_ref[rows, :], stacked, NN, preferred_element_type=F32)
    part = part.reshape(span, chains, OCTET, tile)
    picked = jnp.zeros((chains, OCTET, tile), F32)
    for k, mask in enumerate(octet_masks(ids, span)):
        picked = jnp.where(mask[None], part[k], picked)
    return jnp.sum(picked, axis=1)


def sums_of_window(total_ref, resid, slopes, ids, start, chains, span):
    tile = slopes.shape[1]
    block = chains * OCTET
    rows = pl.ds(pl.multiple_of(start * block, block), span * block)
    spread = jnp.broadcast_to(resid.astype(F32)[:, None, :], (chains, OCTET, tile))
    table = [jnp.where(mask[None], spread, 0.0).reshape(block, tile) for mask in octet_masks(ids, span)]
    table = jnp.concatenate(table, axis=0).astype(BF16)
    total_ref[rows, :] += lax.dot_general(table, slopes, NT, preferred_element_type=F32)


def each_tile(ids_ref, owned, visit, rest):
    octets = owned // OCTET
    span = min(SPAN, octets)
    first = lax.axis_index("loan") * owned
    tiles = ids_ref.shape[1] // TILE
    most = None
    for t in range(tiles):
        ids = ids_ref[:, t * TILE : (t + 1) * TILE] - first
        start, ids = window_of(ids, octets, span)
        visit(t, ids, start, span)
        most = ids if most is None else jnp.maximum(most, ids)

    @pl.when(jnp.max(most) >= span * OCTET)
    def _():
        @pl.loop(0, tiles)
        def _(t):
            cols = pl.ds(pl.multiple_of(t * TILE, TILE), TILE)
            ids = ids_ref[:, cols] - first
            start, _ = window_of(ids, octets, span)

            @pl.loop(start + span, jnp.max(ids) // OCTET + 1)
            def _(q):
                rest(cols, ids - q * OCTET, q)


def all_terms(table_ref, slope_ref, ids_ref, out_ref, chains, owned):
    def visit(t, ids, start, span):
        cols = slice(t * TILE, (t + 1) * TILE)
        out_ref[:, cols] = term_of_window(table_ref, slope_ref[:, cols], ids, start, chains, span)

    def rest(cols, ids, q):
        out_ref[:, cols] += term_of_window(table_ref, slope_ref[:, cols], ids, q, chains, 1)

    each_tile(ids_ref, owned, visit, rest)


def all_sums(total_ref, resid_ref, slope_ref, ids_ref, chains, owned):
    total_ref[...] = jnp.zeros(total_ref.shape, F32)

    def visit(t, ids, start, span):
        cols = slice(t * TILE, (t + 1) * TILE)
        sums_of_window(total_ref, resid_ref[:, cols], slope_ref[:, cols], ids, start, chains, span)

    def rest(cols, ids, q):
        sums_of_window(total_ref, resid_ref[:, cols], slope_ref[:, cols], ids, q, chains, 1)

    each_tile(ids_ref, owned, visit, rest)
    block = chains * OCTET
    return [
        jnp.concatenate(
            [
                total_ref[q * block + c * OCTET : q * block + (c + 1) * OCTET, :]
                for q in range(owned // OCTET)
            ],
            axis=0,
        )
        for c in range(chains)
    ]


def in_vmem(x):
    return pltpu.with_memory_space_constraint(x, pltpu.VMEM)


def in_hbm(x):
    return pltpu.with_memory_space_constraint(x, pltpu.HBM)


def tile_copies(source, target, sems):
    copies = []
    for t in range(source.shape[0] // TILE):
        rows = pl.ds(t * TILE, TILE)
        copies.append(pltpu.make_async_copy(source.at[rows], target.at[rows], sems.at[t]))
    for copy in copies:
        copy.start()
    return copies


def design_scratch(design):
    rows, feats = design.shape
    return [pltpu.VMEM((rows, feats), BF16), pltpu.SemaphoreType.DMA((rows // TILE,))]


def first_logits(design, ids, beta, pools, stride):
    rows, feats = design.shape
    chains, owned, slopes = pools.shape

    def kernel(design_hbm, ids_hbm, beta_hbm, pools_hbm, slope_ref, part_ref, kept, w, table, linear, ids_ref, b_ref, u_ref, sem, sems):
        small = [
            pltpu.make_async_copy(beta_hbm, b_ref, sem.at[0]),
            pltpu.make_async_copy(pools_hbm, u_ref, sem.at[1]),
            pltpu.make_async_copy(ids_hbm, ids_ref, sem.at[2]),
        ]
        for copy in small:
            copy.start()
        size = rows // CHUNKS
        chunks = []
        for k in range(CHUNKS):
            part = pl.ds(k * size, size)
            chunks.append(pltpu.make_async_copy(design_hbm.at[part], kept.at[part], sems.at[k]))
            chunks[k].start()
        g = lax.broadcasted_iota(jnp.int32, (slopes, feats), 0)
        f = lax.broadcasted_iota(jnp.int32, (slopes, feats), 1)
        w[:slopes, :] = jnp.where(f == g * stride, 1.0, 0.0).astype(BF16)
        small[0].wait()
        w[slopes:, :] = b_ref[...].astype(BF16)
        small[1].wait()
        fill_table(table, [u_ref[c] for c in range(chains)])
        small[2].wait()
        for k in range(CHUNKS):
            chunks[k].wait()
            for t in range(k * size // TILE, (k + 1) * size // TILE):
                cols = slice(t * TILE, (t + 1) * TILE)
                both = lax.dot_general(w[...], kept[cols, :], NT, preferred_element_type=F32)
                slope_ref[:, cols] = both[:slopes, :].astype(BF16)
                linear[:, cols] = both[slopes:, :]
        all_terms(table, slope_ref, ids_ref, part_ref, chains, owned)
        part_ref[...] = SCALE * (part_ref[...] + linear[...])

    return pl.pallas_call(
        kernel,
        in_specs=[pl.BlockSpec(memory_space=pl.ANY)] * 4,
        out_specs=[whole(), whole()],
        out_shape=[
            jax.ShapeDtypeStruct((slopes, rows), BF16),
            jax.ShapeDtypeStruct((chains, rows), F32),
        ],
        scratch_shapes=[
            pltpu.VMEM((rows, feats), BF16),
            pltpu.VMEM((slopes + chains, feats), BF16),
            pltpu.VMEM((chains * owned, 2 * slopes), BF16),
            pltpu.VMEM((chains, rows), F32),
            pltpu.VMEM(ids.shape, jnp.int32),
            pltpu.VMEM(beta.shape, F32),
            pltpu.VMEM(pools.shape, F32),
            pltpu.SemaphoreType.DMA((3,)),
            pltpu.SemaphoreType.DMA((CHUNKS,)),
        ],
        compiler_params=params(),
        name="first_logits",
    )(in_hbm(design), in_hbm(ids), in_hbm(beta), in_hbm(pools))


def population_gradient(resid, design):
    def kernel(resid_ref, design_ref, out_ref):
        out_ref[...] = SCALE * lax.dot_general(
            resid_ref[...], design_ref[...], NN, preferred_element_type=F32
        )

    return pl.pallas_call(
        kernel,
        in_specs=[whole(), whole()],
        out_specs=whole(),
        out_shape=jax.ShapeDtypeStruct((resid.shape[0], design.shape[1]), F32),
        compiler_params=params(),
        name="population_gradient",
    )(resid, in_vmem(design))


def stacked_split(x, pieces):
    parts = []
    for _ in range(pieces):
        part = x.astype(BF16)
        parts.append(part)
        x = x - part.astype(F32)
    return jnp.concatenate(parts, axis=0)


def quad(x, j, pairs):
    return jnp.concatenate([x[k] for k in (2 * j, 2 * j + pairs, 2 * j + 1, 2 * j + 1 + pairs)], axis=1)


def region_onehot(index_ref, regions):
    shape = (regions, index_ref.shape[1])
    return jnp.where(lax.broadcasted_iota(jnp.int32, shape, 0) == index_ref[...], 1.0, 0.0)


def chosen_regions(onehot, v):
    chains, _, slopes = v.shape
    pairs = chains // 2
    table = jnp.concatenate([onehot.T.astype(BF16)] * 3, axis=1)
    found = [None] * chains
    for j in range(pairs // 2):
        got = lax.dot_general(
            table, stacked_split(quad(v, j, pairs), 3), NN, preferred_element_type=F32
        )
        for k, c in enumerate((2 * j, 2 * j + pairs, 2 * j + 1, 2 * j + 1 + pairs)):
            found[c] = got[:, k * slopes : (k + 1) * slopes]
    return found


def region_sums(onehot, x, pieces, store):
    pairs = len(x) // 2
    width = 2 * x[0].shape[1]
    table = jnp.concatenate([onehot.astype(BF16)] * pieces, axis=1)
    for j in range(pairs // 2):
        got = lax.dot_general(
            table, stacked_split(quad(x, j, pairs), pieces), NN, preferred_element_type=F32
        )
        store(2 * j, got[:, :width])
        store(2 * j + 1, got[:, width:])


def smem():
    return pl.BlockSpec(memory_space=pltpu.SMEM)


def prior(index, step, pools, regions, momentum, design):
    chains, owned, slopes = pools.shape
    n_regions = regions.shape[1]
    pairs = chains // 2

    def kernel(index_ref, step_ref, pools_ref, regions_ref, mom_ref, design_hbm, base_ref, sums_ref, kept, sem):
        copy = pltpu.make_async_copy(design_hbm, kept, sem)
        copy.start()
        onehot = region_onehot(index_ref, n_regions)
        chosen = chosen_regions(onehot, regions_ref[...])
        dev = [PREC * (pools_ref[c] - chosen[c]) for c in range(chains)]
        for c in range(chains):
            base_ref[c] = mom_ref[c] - (0.5 * step_ref[c]) * dev[c]

        def store(k, value):
            sums_ref[k] = SCALE * value

        region_sums(onehot, dev, 3, store)
        count = jnp.sum(onehot, axis=1, keepdims=True)
        sums_ref[pairs] = SCALE * jnp.broadcast_to(count, (n_regions, 2 * slopes))
        copy.wait()

    return pl.pallas_call(
        kernel,
        in_specs=[whole(), smem(), whole(), whole(), whole(), pl.BlockSpec(memory_space=pl.ANY)],
        out_specs=[whole()] * 3,
        out_shape=[
            jax.ShapeDtypeStruct(pools.shape, F32),
            jax.ShapeDtypeStruct((pairs + 1, n_regions, 2 * slopes), F32),
            pltpu.VMEM(design.shape, BF16),
        ],
        scratch_shapes=[pltpu.SemaphoreType.DMA],
        compiler_params=params(),
        name="prior",
    )(index, step, pools, regions, momentum, in_hbm(design))


def pool_step(resid, slope, ids, index, step, base, mom_base, n_regions):
    chains, owned, slopes = base.shape
    rows = resid.shape[1]
    pairs = chains // 2

    def kernel(resid_ref, slope_ref, ids_ref, index_ref, step_ref, base_ref, mb_ref, next_ref, half_ref, term_ref, sums_ref, table, total):
        lik = all_sums(total, resid_ref, slope_ref, ids_ref, chains, owned)
        way, ahead = [], []
        for c in range(chains):
            half = mb_ref[c] + (0.5 * step_ref[c]) * lik[c]
            half_ref[c] = half
            way.append(step_ref[c] * half)
            ahead.append(base_ref[c] + way[c])
            next_ref[c] = ahead[c]
        fill_table(table, ahead)
        all_terms(table, slope_ref, ids_ref, term_ref, chains, owned)

        def store(k, value):
            sums_ref[k] = SCALE * value

        region_sums(region_onehot(index_ref, n_regions), way, 2, store)

    return pl.pallas_call(
        kernel,
        in_specs=[whole()] * 4 + [smem()] + [whole()] * 2,
        out_specs=[whole()] * 4,
        out_shape=[
            jax.ShapeDtypeStruct(base.shape, F32),
            jax.ShapeDtypeStruct(base.shape, F32),
            jax.ShapeDtypeStruct((chains, rows), F32),
            jax.ShapeDtypeStruct((pairs, n_regions, 2 * slopes), F32),
        ],
        scratch_shapes=[
            pltpu.VMEM((chains * owned, 2 * slopes), BF16),
            pltpu.VMEM((chains * owned, slopes), F32),
        ],
        compiler_params=params(),
        name="pool_step",
    )(resid, slope, ids, index, step, base, mom_base)


def region_step(index, step, sums, regions, momentum, pool_part):
    chains, owned, slopes = pool_part.shape
    n_regions = regions.shape[1]
    pairs = chains // 2

    def kernel(index_ref, step_ref, sums_ref, v_ref, m_ref, part_ref, next_ref, mom_ref, pool_ref):
        def part(k, c):
            side = slice((c // pairs) * slopes, (c // pairs + 1) * slopes)
            return (1.0 / SCALE) * sums_ref[k + c % pairs][:, side]

        count = (1.0 / SCALE) * sums_ref[pairs][:, :slopes]
        for c in range(chains):
            v, h = v_ref[c], 0.5 * step_ref[c]
            dev = part(0, c)
            half = m_ref[c] + h * (dev - PREC * v)
            ahead = v + step_ref[c] * half
            next_ref[c] = ahead
            gain = dev + PREC * (part(pairs + 1, c) - count * (ahead - v)) - PREC * ahead
            mom_ref[c] = half + h * gain
        chosen = chosen_regions(region_onehot(index_ref, n_regions), next_ref[...])
        for c in range(chains):
            pool_ref[c] = part_ref[c] + (0.5 * step_ref[c]) * (PREC * chosen[c])

    return pl.pallas_call(
        kernel,
        in_specs=[whole(), smem()] + [whole()] * 4,
        out_specs=[whole()] * 3,
        out_shape=[
            jax.ShapeDtypeStruct(regions.shape, F32),
            jax.ShapeDtypeStruct(regions.shape, F32),
            jax.ShapeDtypeStruct(pool_part.shape, F32),
        ],
        compiler_params=params(),
        name="region_step",
    )(index, step, sums, regions, momentum, pool_part)


def pool_likelihood(resid, slope, ids, step, half, pools_next):
    chains, owned, slopes = half.shape

    def kernel(resid_ref, slope_ref, ids_ref, step_ref, half_ref, u_ref, out_ref, total):
        lik = all_sums(total, resid_ref, slope_ref, ids_ref, chains, owned)
        for c in range(chains):
            out_ref[c] = half_ref[c] + (0.5 * step_ref[c]) * (lik[c] - PREC * u_ref[c])

    return pl.pallas_call(
        kernel,
        in_specs=[whole()] * 3 + [smem(), whole(), whole()],
        out_specs=whole(),
        out_shape=jax.ShapeDtypeStruct(half.shape, F32),
        scratch_shapes=[pltpu.VMEM((chains * owned, slopes), F32)],
        compiler_params=params(),
        name="pool_likelihood",
    )(resid, slope, ids, step, half, pools_next)


def next_logits(design, coef, term):
    rows = design.shape[0]

    def kernel(design_ref, coef_ref, term_ref, out_ref):
        coef16 = coef_ref[...].astype(BF16)
        for t in range(rows // TILE):
            cols = slice(t * TILE, (t + 1) * TILE)
            linear = lax.dot_general(coef16, design_ref[cols, :], NT, preferred_element_type=F32)
            out_ref[:, cols] = SCALE * (term_ref[:, cols] + linear)

    return pl.pallas_call(
        kernel,
        in_specs=[whole(), whole(), whole()],
        out_specs=whole(),
        out_shape=jax.ShapeDtypeStruct(term.shape, F32),
        compiler_params=params(),
        name="next_logits",
    )(in_vmem(design), coef, term)


def ahead_by(k, size, stride, group):
    perm = []
    for i in range(size):
        digit = (i // stride) % group
        perm.append((i, i + ((digit + k) % group - digit) * stride))
    return perm


def total_over(x, axis):
    size = lax.axis_size(axis)
    stride = 1
    while stride < size:
        group = min(4, size // stride)
        own = lax.optimization_barrier(x.astype(jnp.float16))
        parts = [own] + [
            lax.ppermute(own, axis, ahead_by(k, size, stride, group)) for k in range(1, group)
        ]
        parts = [p.astype(F32) for p in parts]
        x = parts[0] + parts[1] if group == 2 else (parts[0] + parts[2]) + (parts[1] + parts[3])
        stride *= group
    return x


def shared_sum(x, axis):
    size = lax.axis_size(axis)
    me = lax.axis_index(axis)
    width = x.shape[1] // size
    x = lax.optimization_barrier(x.astype(jnp.float16))

    def block(k):
        return lax.dynamic_slice_in_dim(x, lax.rem(me + k, size) * width, width, 1)

    mine = block(0).astype(F32)
    for k in range(1, size):
        mine = mine + lax.ppermute(block(k), axis, ahead_by(k, size, 1, size)).astype(F32)
    mine = lax.optimization_barrier(mine.astype(jnp.float16))
    found = [mine] + [lax.ppermute(mine, axis, ahead_by(k, size, 1, size)) for k in range(1, size)]
    back = jnp.concatenate(found[::-1], axis=1)
    return jnp.roll(back, (me + 1) * width, axis=1).astype(F32)


def residual(part, labels):
    logit = total_over(part, "feat") * (1.0 / SCALE)
    return (labels.astype(F32)[None, :] - jax.nn.sigmoid(logit)).astype(BF16)


def body(
    design,
    labels,
    pool_ids,
    pool_region_index,
    step_size,
    beta,
    pools,
    regions,
    beta_momentum,
    pool_momentum,
    region_momentum,
):
    rows, feats = design.shape
    chains, owned, slopes = pools.shape
    n_regions = regions.shape[1]
    total_feats = float(feats * lax.axis_size("feat"))
    half = 0.5 * step_size
    ids = pool_ids[None, :]
    index = pool_region_index[None, :]

    slope, part = first_logits(design, ids, beta, pools, feats // slopes)
    pools_at, part = lax.optimization_barrier((pools, part))
    mom_base, dev_sums, kept = prior(
        index, step_size, pools_at, regions, pool_momentum, design
    )

    resid = residual(part, labels)
    gb = population_gradient(resid, kept)
    resid, gb, mom_base, dev_sums = lax.optimization_barrier((resid, gb, mom_base, dev_sums))
    pools_next, pool_half, term, way_sums = pool_step(
        resid, slope, ids, index, step_size, pools, mom_base, n_regions
    )
    sums = shared_sum(jnp.concatenate([dev_sums, way_sums], axis=0), "loan")
    gb = total_over(gb, "loan") * (1.0 / SCALE) - total_feats * beta
    beta_half = beta_momentum + half[:, None] * gb
    beta_next = beta + step_size[:, None] * beta_half

    part = next_logits(design, beta_next, term)
    resid = residual(part, labels)
    gb = population_gradient(resid, design)
    resid, gb = lax.optimization_barrier((resid, gb))
    pool_part = pool_likelihood(resid, slope, ids, step_size, pool_half, pools_next)
    regions_next, region_out, pool_out = region_step(
        index, step_size, sums, regions, region_momentum, pool_part
    )
    gb = total_over(gb, "loan") * (1.0 / SCALE) - total_feats * beta_next
    beta_out = beta_half + half[:, None] * gb
    return (beta_next, pools_next, regions_next, beta_out, pool_out, region_out)


def solution(mesh):
    in_specs = (
        P(("grp", "loan"), "feat"),
        P(("grp", "loan")),
        P(("grp", "loan")),
        P(("grp", "loan")),
        P("grp"),
        P("grp", "feat"),
        P("grp", "loan", "feat"),
        P("grp", None, "feat"),
        P("grp", "feat"),
        P("grp", "loan", "feat"),
        P("grp", None, "feat"),
    )
    out_specs = (
        P("grp", "feat"),
        P("grp", "loan", "feat"),
        P("grp", None, "feat"),
        P("grp", "feat"),
        P("grp", "loan", "feat"),
        P("grp", None, "feat"),
    )
    return jax.shard_map(body, mesh=mesh, in_specs=in_specs, out_specs=out_specs, check_vma=False)
```

```python
import jax
import jax.numpy as jnp
from jax import lax
from jax.experimental import pallas as pl
from jax.experimental.pallas import tpu as pltpu
from jax.sharding import PartitionSpec as P

PREC = 256.0
SCALE = 1.0 / 16.0
TILE = 256
OCTET = 8
SPAN = 3
CHUNKS = 2
LANES = 128
COPIES = 1
VMEM_LIMIT = 24 * 1024 * 1024
NT = (((1,), (1,)), ((), ()))
NN = (((1,), (0,)), ((), ()))
F32 = jnp.float32
BF16 = jnp.bfloat16


def whole():
    return pl.BlockSpec(memory_space=pltpu.VMEM)


def params():
    return pltpu.CompilerParams(vmem_limit_bytes=VMEM_LIMIT)


def fill_table(table_ref, u):
    chains, octets = len(u), u[0].shape[0] // OCTET
    for q in range(octets):
        rows = jnp.concatenate([x[q * OCTET : (q + 1) * OCTET, :] for x in u], axis=0)
        high = rows.astype(BF16)
        low = (rows - high.astype(F32)).astype(BF16)
        table_ref[q * chains * OCTET : (q + 1) * chains * OCTET, :] = jnp.concatenate([high, low], axis=1)


def window_of(ids, octets, span):
    start = jnp.clip(jnp.min(ids) // OCTET, 0, octets - span)
    return start, ids - start * OCTET


def octet_masks(ids, span):
    sub = lax.broadcasted_iota(jnp.int32, (OCTET, ids.shape[1]), 0)
    return [sub + OCTET * k == ids for k in range(span)]


def term_of_window(table_ref, slopes, ids, start, chains, span):
    tile = slopes.shape[1]
    block = chains * OCTET
    rows = pl.ds(pl.multiple_of(start * block, block), span * block)
    stacked = jnp.concatenate([slopes, slopes], axis=0)
    part = lax.dot_general(table_ref[rows, :], stacked, NN, preferred_element_type=F32)
    part = part.reshape(span, chains, OCTET, tile)
    picked = jnp.zeros((chains, OCTET, tile), F32)
    for k, mask in enumerate(octet_masks(ids, span)):
        picked = jnp.where(mask[None], part[k], picked)
    return jnp.sum(picked, axis=1)


def sums_of_window(total_ref, resid, slopes, ids, start, chains, span):
    tile = slopes.shape[1]
    block = chains * OCTET
    rows = pl.ds(pl.multiple_of(start * block, block), span * block)
    spread = jnp.broadcast_to(resid.astype(F32)[:, None, :], (chains, OCTET, tile))
    table = [jnp.where(mask[None], spread, 0.0).reshape(block, tile) for mask in octet_masks(ids, span)]
    table = jnp.concatenate(table, axis=0).astype(BF16)
    total_ref[rows, :] += lax.dot_general(table, slopes, NT, preferred_element_type=F32)


def each_tile(ids_ref, owned, visit, rest):
    octets = owned // OCTET
    span = min(SPAN, octets)
    first = lax.axis_index("loan") * owned
    tiles = ids_ref.shape[1] // TILE
    most = None
    for t in range(tiles):
        ids = ids_ref[:, t * TILE : (t + 1) * TILE] - first
        start, ids = window_of(ids, octets, span)
        visit(t, ids, start, span)
        most = ids if most is None else jnp.maximum(most, ids)

    @pl.when(jnp.max(most) >= span * OCTET)
    def _():
        @pl.loop(0, tiles)
        def _(t):
            cols = pl.ds(pl.multiple_of(t * TILE, TILE), TILE)
            ids = ids_ref[:, cols] - first
            start, _ = window_of(ids, octets, span)

            @pl.loop(start + span, jnp.max(ids) // OCTET + 1)
            def _(q):
                rest(cols, ids - q * OCTET, q)


def all_terms(table_ref, slope_ref, ids_ref, out_ref, chains, owned):
    def visit(t, ids, start, span):
        cols = slice(t * TILE, (t + 1) * TILE)
        out_ref[:, cols] = term_of_window(table_ref, slope_ref[:, cols], ids, start, chains, span)

    def rest(cols, ids, q):
        out_ref[:, cols] += term_of_window(table_ref, slope_ref[:, cols], ids, q, chains, 1)

    each_tile(ids_ref, owned, visit, rest)


def all_sums(total_ref, resid_ref, slope_ref, ids_ref, chains, owned):
    total_ref[...] = jnp.zeros(total_ref.shape, F32)

    def visit(t, ids, start, span):
        cols = slice(t * TILE, (t + 1) * TILE)
        sums_of_window(total_ref, resid_ref[:, cols], slope_ref[:, cols], ids, start, chains, span)

    def rest(cols, ids, q):
        sums_of_window(total_ref, resid_ref[:, cols], slope_ref[:, cols], ids, q, chains, 1)

    each_tile(ids_ref, owned, visit, rest)
    block = chains * OCTET
    return [
        jnp.concatenate(
            [
                total_ref[q * block + c * OCTET : q * block + (c + 1) * OCTET, :]
                for q in range(owned // OCTET)
            ],
            axis=0,
        )
        for c in range(chains)
    ]


def in_vmem(x):
    return pltpu.with_memory_space_constraint(x, pltpu.VMEM)


def in_hbm(x):
    return pltpu.with_memory_space_constraint(x, pltpu.HBM)


def tile_copies(source, target, sems):
    copies = []
    for t in range(source.shape[0] // TILE):
        rows = pl.ds(t * TILE, TILE)
        copies.append(pltpu.make_async_copy(source.at[rows], target.at[rows], sems.at[t]))
    for copy in copies:
        copy.start()
    return copies


def design_scratch(design):
    rows, feats = design.shape
    return [pltpu.VMEM((rows, feats), BF16), pltpu.SemaphoreType.DMA((rows // TILE,))]


def first_logits(design, ids, beta, pools, stride):
    rows, feats = design.shape
    chains, owned, slopes = pools.shape

    def kernel(design_hbm, ids_hbm, beta_hbm, pools_hbm, slope_ref, part_ref, kept, w, table, linear, ids_ref, b_ref, u_ref, sem, sems):
        small = [
            pltpu.make_async_copy(beta_hbm, b_ref, sem.at[0]),
            pltpu.make_async_copy(pools_hbm, u_ref, sem.at[1]),
            pltpu.make_async_copy(ids_hbm, ids_ref, sem.at[2]),
        ]
        for copy in small:
            copy.start()
        size = rows // CHUNKS
        chunks = []
        for k in range(CHUNKS):
            part = pl.ds(k * size, size)
            chunks.append(pltpu.make_async_copy(design_hbm.at[part], kept.at[part], sems.at[k]))
            chunks[k].start()
        g = lax.broadcasted_iota(jnp.int32, (slopes, feats), 0)
        f = lax.broadcasted_iota(jnp.int32, (slopes, feats), 1)
        w[:slopes, :] = jnp.where(f == g * stride, 1.0, 0.0).astype(BF16)
        small[0].wait()
        w[slopes:, :] = b_ref[...].astype(BF16)
        small[1].wait()
        fill_table(table, [u_ref[c] for c in range(chains)])
        small[2].wait()
        for k in range(CHUNKS):
            chunks[k].wait()
            for t in range(k * size // TILE, (k + 1) * size // TILE):
                cols = slice(t * TILE, (t + 1) * TILE)
                both = lax.dot_general(w[...], kept[cols, :], NT, preferred_element_type=F32)
                slope_ref[:, cols] = both[:slopes, :].astype(BF16)
                linear[:, cols] = both[slopes:, :]
        all_terms(table, slope_ref, ids_ref, part_ref, chains, owned)
        part_ref[...] = SCALE * (part_ref[...] + linear[...])

    return pl.pallas_call(
        kernel,
        in_specs=[pl.BlockSpec(memory_space=pl.ANY)] * 4,
        out_specs=[whole(), whole()],
        out_shape=[
            jax.ShapeDtypeStruct((slopes, rows), BF16),
            jax.ShapeDtypeStruct((chains, rows), F32),
        ],
        scratch_shapes=[
            pltpu.VMEM((rows, feats), BF16),
            pltpu.VMEM((slopes + chains, feats), BF16),
            pltpu.VMEM((chains * owned, 2 * slopes), BF16),
            pltpu.VMEM((chains, rows), F32),
            pltpu.VMEM(ids.shape, jnp.int32),
            pltpu.VMEM(beta.shape, F32),
            pltpu.VMEM(pools.shape, F32),
            pltpu.SemaphoreType.DMA((3,)),
            pltpu.SemaphoreType.DMA((CHUNKS,)),
        ],
        compiler_params=params(),
        name="first_logits",
    )(in_hbm(design), in_hbm(ids), in_hbm(beta), in_hbm(pools))


def population_gradient(resid, design):
    planes = design.shape[1] // LANES

    def kernel(resid_ref, design_ref, out_ref):
        total = SCALE * lax.dot_general(
            resid_ref[...], design_ref[...], NN, preferred_element_type=F32
        )
        for k in range(planes):
            out_ref[k] = total[:, k * LANES : (k + 1) * LANES]

    return pl.pallas_call(
        kernel,
        in_specs=[whole(), whole()],
        out_specs=whole(),
        out_shape=jax.ShapeDtypeStruct((planes, resid.shape[0], LANES), F32),
        compiler_params=params(),
        name="population_gradient",
    )(resid, in_vmem(design))


def stacked_split(x, pieces):
    parts = []
    for _ in range(pieces):
        part = x.astype(BF16)
        parts.append(part)
        x = x - part.astype(F32)
    return jnp.concatenate(parts, axis=0)


def quad(x, j, pairs):
    return jnp.concatenate([x[k] for k in (2 * j, 2 * j + pairs, 2 * j + 1, 2 * j + 1 + pairs)], axis=1)


def region_onehot(index_ref, regions):
    shape = (regions, index_ref.shape[1])
    return jnp.where(lax.broadcasted_iota(jnp.int32, shape, 0) == index_ref[...], 1.0, 0.0)


def chosen_regions(onehot, v):
    chains, _, slopes = v.shape
    pairs = chains // 2
    table = jnp.concatenate([onehot.T.astype(BF16)] * 3, axis=1)
    found = [None] * chains
    for j in range(pairs // 2):
        got = lax.dot_general(
            table, stacked_split(quad(v, j, pairs), 3), NN, preferred_element_type=F32
        )
        for k, c in enumerate((2 * j, 2 * j + pairs, 2 * j + 1, 2 * j + 1 + pairs)):
            found[c] = got[:, k * slopes : (k + 1) * slopes]
    return found


def region_sums(onehot, x, pieces, store):
    pairs = len(x) // 2
    width = 2 * x[0].shape[1]
    table = jnp.concatenate([onehot.astype(BF16)] * pieces, axis=1)
    for j in range(pairs // 2):
        got = lax.dot_general(
            table, stacked_split(quad(x, j, pairs), pieces), NN, preferred_element_type=F32
        )
        store(2 * j, got[:, :width])
        store(2 * j + 1, got[:, width:])


def smem():
    return pl.BlockSpec(memory_space=pltpu.SMEM)


def prior(index, step, pools, regions, momentum, design):
    chains, owned, slopes = pools.shape
    n_regions = regions.shape[1]
    pairs = chains // 2

    def kernel(index_ref, step_ref, pools_ref, regions_ref, mom_ref, design_hbm, base_ref, sums_ref, kept, sems):
        size = design_hbm.shape[0] // COPIES
        copies = []
        for k in range(COPIES):
            part = pl.ds(k * size, size)
            copies.append(pltpu.make_async_copy(design_hbm.at[part], kept.at[part], sems.at[k]))
            copies[k].start()
        onehot = region_onehot(index_ref, n_regions)
        chosen = chosen_regions(onehot, regions_ref[...])
        dev = [PREC * (pools_ref[c] - chosen[c]) for c in range(chains)]
        for c in range(chains):
            base_ref[c] = mom_ref[c] - (0.5 * step_ref[c]) * dev[c]

        def store(k, value):
            sums_ref[k] = SCALE * value

        region_sums(onehot, dev, 3, store)
        count = jnp.sum(onehot, axis=1, keepdims=True)
        sums_ref[pairs] = SCALE * jnp.broadcast_to(count, (n_regions, 2 * slopes))
        for copy in copies:
            copy.wait()

    return pl.pallas_call(
        kernel,
        in_specs=[whole(), smem(), whole(), whole(), whole(), pl.BlockSpec(memory_space=pl.ANY)],
        out_specs=[whole()] * 3,
        out_shape=[
            jax.ShapeDtypeStruct(pools.shape, F32),
            jax.ShapeDtypeStruct((pairs + 1, n_regions, 2 * slopes), F32),
            pltpu.VMEM(design.shape, BF16),
        ],
        scratch_shapes=[pltpu.SemaphoreType.DMA((COPIES,))],
        compiler_params=params(),
        name="prior",
    )(index, step, pools, regions, momentum, in_hbm(design))


def pool_step(resid, slope, ids, index, step, base, mom_base, n_regions):
    chains, owned, slopes = base.shape
    rows = resid.shape[1]
    pairs = chains // 2

    def kernel(resid_ref, slope_ref, ids_ref, index_ref, step_ref, base_ref, mb_ref, next_ref, half_ref, term_ref, sums_ref, table, total):
        lik = all_sums(total, resid_ref, slope_ref, ids_ref, chains, owned)
        way, ahead = [], []
        for c in range(chains):
            half = mb_ref[c] + (0.5 * step_ref[c]) * lik[c]
            half_ref[c] = half
            way.append(step_ref[c] * half)
            ahead.append(base_ref[c] + way[c])
            next_ref[c] = ahead[c]
        fill_table(table, ahead)
        all_terms(table, slope_ref, ids_ref, term_ref, chains, owned)

        def store(k, value):
            sums_ref[k] = SCALE * value

        region_sums(region_onehot(index_ref, n_regions), way, 2, store)

    return pl.pallas_call(
        kernel,
        in_specs=[whole()] * 4 + [smem()] + [whole()] * 2,
        out_specs=[whole()] * 4,
        out_shape=[
            jax.ShapeDtypeStruct(base.shape, F32),
            jax.ShapeDtypeStruct(base.shape, F32),
            jax.ShapeDtypeStruct((chains, rows), F32),
            jax.ShapeDtypeStruct((pairs, n_regions, 2 * slopes), F32),
        ],
        scratch_shapes=[
            pltpu.VMEM((chains * owned, 2 * slopes), BF16),
            pltpu.VMEM((chains * owned, slopes), F32),
        ],
        compiler_params=params(),
        name="pool_step",
    )(resid, slope, ids, index, step, base, mom_base)


def region_step(index, step, sums, regions, momentum, pool_part):
    chains, owned, slopes = pool_part.shape
    n_regions = regions.shape[1]
    pairs = chains // 2

    def kernel(index_ref, step_ref, sums_ref, v_ref, m_ref, part_ref, next_ref, mom_ref, pool_ref):
        def part(k, c):
            side = slice((c // pairs) * slopes, (c // pairs + 1) * slopes)
            return (1.0 / SCALE) * sums_ref[k + c % pairs][:, side]

        count = (1.0 / SCALE) * sums_ref[pairs][:, :slopes]
        for c in range(chains):
            v, h = v_ref[c], 0.5 * step_ref[c]
            dev = part(0, c)
            half = m_ref[c] + h * (dev - PREC * v)
            ahead = v + step_ref[c] * half
            next_ref[c] = ahead
            gain = dev + PREC * (part(pairs + 1, c) - count * (ahead - v)) - PREC * ahead
            mom_ref[c] = half + h * gain
        chosen = chosen_regions(region_onehot(index_ref, n_regions), next_ref[...])
        for c in range(chains):
            pool_ref[c] = part_ref[c] + (0.5 * step_ref[c]) * (PREC * chosen[c])

    return pl.pallas_call(
        kernel,
        in_specs=[whole(), smem()] + [whole()] * 4,
        out_specs=[whole()] * 3,
        out_shape=[
            jax.ShapeDtypeStruct(regions.shape, F32),
            jax.ShapeDtypeStruct(regions.shape, F32),
            jax.ShapeDtypeStruct(pool_part.shape, F32),
        ],
        compiler_params=params(),
        name="region_step",
    )(index, step, sums, regions, momentum, pool_part)


def pool_likelihood(resid, slope, ids, step, half, pools_next):
    chains, owned, slopes = half.shape

    def kernel(resid_ref, slope_ref, ids_ref, step_ref, half_ref, u_ref, out_ref, total):
        lik = all_sums(total, resid_ref, slope_ref, ids_ref, chains, owned)
        for c in range(chains):
            out_ref[c] = half_ref[c] + (0.5 * step_ref[c]) * (lik[c] - PREC * u_ref[c])

    return pl.pallas_call(
        kernel,
        in_specs=[whole()] * 3 + [smem(), whole(), whole()],
        out_specs=whole(),
        out_shape=jax.ShapeDtypeStruct(half.shape, F32),
        scratch_shapes=[pltpu.VMEM((chains * owned, slopes), F32)],
        compiler_params=params(),
        name="pool_likelihood",
    )(resid, slope, ids, step, half, pools_next)


def next_logits(design, coef, term):
    rows = design.shape[0]

    def kernel(design_ref, coef_ref, term_ref, out_ref):
        coef16 = coef_ref[...].astype(BF16)
        for t in range(rows // TILE):
            cols = slice(t * TILE, (t + 1) * TILE)
            linear = lax.dot_general(coef16, design_ref[cols, :], NT, preferred_element_type=F32)
            out_ref[:, cols] = SCALE * (term_ref[:, cols] + linear)

    return pl.pallas_call(
        kernel,
        in_specs=[whole(), whole(), whole()],
        out_specs=whole(),
        out_shape=jax.ShapeDtypeStruct(term.shape, F32),
        compiler_params=params(),
        name="next_logits",
    )(in_vmem(design), coef, term)


def ahead_by(k, size, stride, group):
    perm = []
    for i in range(size):
        digit = (i // stride) % group
        perm.append((i, i + ((digit + k) % group - digit) * stride))
    return perm


def total_over(x, axis):
    size = lax.axis_size(axis)
    stride = 1
    while stride < size:
        group = min(4, size // stride)
        own = lax.optimization_barrier(x.astype(jnp.float16))
        parts = [own] + [
            lax.ppermute(own, axis, ahead_by(k, size, stride, group)) for k in range(1, group)
        ]
        parts = [p.astype(F32) for p in parts]
        x = parts[0] + parts[1] if group == 2 else (parts[0] + parts[2]) + (parts[1] + parts[3])
        stride *= group
    return x


def own_block(x, axis):
    size = lax.axis_size(axis)
    me = lax.axis_index(axis)
    width = x.shape[1] // size
    x = lax.optimization_barrier(x.astype(jnp.float16))

    def block(k):
        return lax.dynamic_slice_in_dim(x, lax.rem(me + k, size) * width, width, 1)

    mine = block(0).astype(F32)
    for k in range(1, size):
        mine = mine + lax.ppermute(block(k), axis, ahead_by(k, size, 1, size)).astype(F32)
    return mine.astype(jnp.float16)


def all_shifts(x, axis):
    size = lax.axis_size(axis)
    x = lax.optimization_barrier(x)
    return [x] + [lax.ppermute(x, axis, ahead_by(k, size, 1, size)) for k in range(1, size)]


def in_order(parts, axis):
    size = lax.axis_size(axis)
    me = lax.axis_index(axis)
    width = parts[0].shape[1]
    found = jnp.zeros((parts[0].shape[0], size * width) + parts[0].shape[2:], parts[0].dtype)
    for k, part in enumerate(parts):
        at = lax.rem(me + size - k, size) * width
        found = lax.dynamic_update_slice_in_dim(found, part, at, 1)
    return found.astype(F32)


def total_and_blocks(gb, mine, axis):
    size = lax.axis_size(axis)
    if size > 4 or mine.shape[1] != gb.shape[1] or mine.shape[2] != gb.shape[2]:
        return total_over(gb, axis), in_order(all_shifts(mine, axis), axis)
    planes = gb.shape[0]
    parts = all_shifts(jnp.concatenate([gb.astype(jnp.float16), mine], axis=0), axis)
    g = [part[:planes].astype(F32) for part in parts]
    total = g[0] if size == 1 else g[0] + g[1] if size == 2 else (g[0] + g[2]) + (g[1] + g[3])
    return total, in_order([part[planes:] for part in parts], axis)


def flat(planes):
    return jnp.concatenate(list(planes), axis=1)


def residual(part, labels):
    logit = total_over(part, "feat") * (1.0 / SCALE)
    return (labels.astype(F32)[None, :] - jax.nn.sigmoid(logit)).astype(BF16)


def body(
    design,
    labels,
    pool_ids,
    pool_region_index,
    step_size,
    beta,
    pools,
    regions,
    beta_momentum,
    pool_momentum,
    region_momentum,
):
    rows, feats = design.shape
    chains, owned, slopes = pools.shape
    n_regions = regions.shape[1]
    total_feats = float(feats * lax.axis_size("feat"))
    half = 0.5 * step_size
    ids = pool_ids[None, :]
    index = pool_region_index[None, :]

    slope, part = first_logits(design, ids, beta, pools, feats // slopes)
    pools_at, part = lax.optimization_barrier((pools, part))
    mom_base, dev_sums, kept = prior(
        index, step_size, pools_at, regions, pool_momentum, design
    )

    resid = residual(part, labels)
    gb = population_gradient(resid, kept)
    resid, gb, mom_base, dev_sums = lax.optimization_barrier((resid, gb, mom_base, dev_sums))
    pools_next, pool_half, term, way_sums = pool_step(
        resid, slope, ids, index, step_size, pools, mom_base, n_regions
    )
    mine = own_block(jnp.concatenate([dev_sums, way_sums], axis=0), "loan")
    gb = flat(total_over(gb, "loan")) * (1.0 / SCALE) - total_feats * beta
    beta_half = beta_momentum + half[:, None] * gb
    beta_next = beta + step_size[:, None] * beta_half

    part = next_logits(design, beta_next, term)
    resid = residual(part, labels)
    gb = population_gradient(resid, design)
    resid, gb = lax.optimization_barrier((resid, gb))
    pool_part = pool_likelihood(resid, slope, ids, step_size, pool_half, pools_next)
    gb, sums = total_and_blocks(gb, mine, "loan")
    regions_next, region_out, pool_out = region_step(
        index, step_size, sums, regions, region_momentum, pool_part
    )
    gb = flat(gb) * (1.0 / SCALE) - total_feats * beta_next
    beta_out = beta_half + half[:, None] * gb
    return (beta_next, pools_next, regions_next, beta_out, pool_out, region_out)


def solution(mesh):
    in_specs = (
        P(("grp", "loan"), "feat"),
        P(("grp", "loan")),
        P(("grp", "loan")),
        P(("grp", "loan")),
        P("grp"),
        P("grp", "feat"),
        P("grp", "loan", "feat"),
        P("grp", None, "feat"),
        P("grp", "feat"),
        P("grp", "loan", "feat"),
        P("grp", None, "feat"),
    )
    out_specs = (
        P("grp", "feat"),
        P("grp", "loan", "feat"),
        P("grp", None, "feat"),
        P("grp", "feat"),
        P("grp", "loan", "feat"),
        P("grp", None, "feat"),
    )
    return jax.shard_map(body, mesh=mesh, in_specs=in_specs, out_specs=out_specs, check_vma=False)
```

```python
import jax
import jax.numpy as jnp
from jax import lax
from jax.experimental import pallas as pl
from jax.experimental.pallas import tpu as pltpu
from jax.sharding import PartitionSpec as P

PREC = 256.0
SCALE = 1.0 / 16.0
TILE = 256
OCTET = 8
SPAN = 3
CHUNKS = 2
LANES = 128
COPIES = 1
VMEM_LIMIT = 24 * 1024 * 1024
NT = (((1,), (1,)), ((), ()))
NN = (((1,), (0,)), ((), ()))
F32 = jnp.float32
BF16 = jnp.bfloat16


def whole():
    return pl.BlockSpec(memory_space=pltpu.VMEM)


def params():
    return pltpu.CompilerParams(vmem_limit_bytes=VMEM_LIMIT)


def fill_table(table_ref, u):
    chains, octets = len(u), u[0].shape[0] // OCTET
    for q in range(octets):
        rows = jnp.concatenate([x[q * OCTET : (q + 1) * OCTET, :] for x in u], axis=0)
        high = rows.astype(BF16)
        low = (rows - high.astype(F32)).astype(BF16)
        table_ref[q * chains * OCTET : (q + 1) * chains * OCTET, :] = jnp.concatenate([high, low], axis=1)


def window_of(ids, octets, span):
    start = jnp.clip(jnp.min(ids) // OCTET, 0, octets - span)
    return start, ids - start * OCTET


def octet_masks(ids, span):
    sub = lax.broadcasted_iota(jnp.int32, (OCTET, ids.shape[1]), 0)
    return [sub + OCTET * k == ids for k in range(span)]


def term_of_window(table_ref, slopes, ids, start, chains, span):
    tile = slopes.shape[1]
    block = chains * OCTET
    rows = pl.ds(pl.multiple_of(start * block, block), span * block)
    stacked = jnp.concatenate([slopes, slopes], axis=0)
    part = lax.dot_general(table_ref[rows, :], stacked, NN, preferred_element_type=F32)
    part = part.reshape(span, chains, OCTET, tile)
    picked = jnp.zeros((chains, OCTET, tile), F32)
    for k, mask in enumerate(octet_masks(ids, span)):
        picked = jnp.where(mask[None], part[k], picked)
    return jnp.sum(picked, axis=1)


def sums_of_window(total_ref, resid, slopes, ids, start, chains, span):
    tile = slopes.shape[1]
    block = chains * OCTET
    rows = pl.ds(pl.multiple_of(start * block, block), span * block)
    spread = jnp.broadcast_to(resid.astype(F32)[:, None, :], (chains, OCTET, tile))
    table = [jnp.where(mask[None], spread, 0.0).reshape(block, tile) for mask in octet_masks(ids, span)]
    table = jnp.concatenate(table, axis=0).astype(BF16)
    total_ref[rows, :] += lax.dot_general(table, slopes, NT, preferred_element_type=F32)


def each_tile(ids_ref, owned, visit, rest):
    octets = owned // OCTET
    span = min(SPAN, octets)
    first = lax.axis_index("loan") * owned
    tiles = ids_ref.shape[1] // TILE
    most = None
    for t in range(tiles):
        ids = ids_ref[:, t * TILE : (t + 1) * TILE] - first
        start, ids = window_of(ids, octets, span)
        visit(t, ids, start, span)
        most = ids if most is None else jnp.maximum(most, ids)

    @pl.when(jnp.max(most) >= span * OCTET)
    def _():
        @pl.loop(0, tiles)
        def _(t):
            cols = pl.ds(pl.multiple_of(t * TILE, TILE), TILE)
            ids = ids_ref[:, cols] - first
            start, _ = window_of(ids, octets, span)

            @pl.loop(start + span, jnp.max(ids) // OCTET + 1)
            def _(q):
                rest(cols, ids - q * OCTET, q)


def all_terms(table_ref, slope_ref, ids_ref, out_ref, chains, owned):
    def visit(t, ids, start, span):
        cols = slice(t * TILE, (t + 1) * TILE)
        out_ref[:, cols] = term_of_window(table_ref, slope_ref[:, cols], ids, start, chains, span)

    def rest(cols, ids, q):
        out_ref[:, cols] += term_of_window(table_ref, slope_ref[:, cols], ids, q, chains, 1)

    each_tile(ids_ref, owned, visit, rest)


def all_sums(total_ref, resid_ref, slope_ref, ids_ref, chains, owned):
    total_ref[...] = jnp.zeros(total_ref.shape, F32)

    def visit(t, ids, start, span):
        cols = slice(t * TILE, (t + 1) * TILE)
        sums_of_window(total_ref, resid_ref[:, cols], slope_ref[:, cols], ids, start, chains, span)

    def rest(cols, ids, q):
        sums_of_window(total_ref, resid_ref[:, cols], slope_ref[:, cols], ids, q, chains, 1)

    each_tile(ids_ref, owned, visit, rest)
    block = chains * OCTET
    return [
        jnp.concatenate(
            [
                total_ref[q * block + c * OCTET : q * block + (c + 1) * OCTET, :]
                for q in range(owned // OCTET)
            ],
            axis=0,
        )
        for c in range(chains)
    ]


def in_vmem(x):
    return pltpu.with_memory_space_constraint(x, pltpu.VMEM)


def in_hbm(x):
    return pltpu.with_memory_space_constraint(x, pltpu.HBM)


def tile_copies(source, target, sems):
    copies = []
    for t in range(source.shape[0] // TILE):
        rows = pl.ds(t * TILE, TILE)
        copies.append(pltpu.make_async_copy(source.at[rows], target.at[rows], sems.at[t]))
    for copy in copies:
        copy.start()
    return copies


def design_scratch(design):
    rows, feats = design.shape
    return [pltpu.VMEM((rows, feats), BF16), pltpu.SemaphoreType.DMA((rows // TILE,))]


def first_logits(design, ids, beta, pools, stride):
    rows, feats = design.shape
    chains, owned, slopes = pools.shape

    def kernel(design_hbm, ids_hbm, beta_hbm, pools_hbm, slope_ref, part_ref, kept, w, table, linear, ids_ref, b_ref, u_ref, sem, sems):
        small = [
            pltpu.make_async_copy(beta_hbm, b_ref, sem.at[0]),
            pltpu.make_async_copy(pools_hbm, u_ref, sem.at[1]),
            pltpu.make_async_copy(ids_hbm, ids_ref, sem.at[2]),
        ]
        for copy in small:
            copy.start()
        size = rows // CHUNKS
        chunks = []
        for k in range(CHUNKS):
            part = pl.ds(k * size, size)
            chunks.append(pltpu.make_async_copy(design_hbm.at[part], kept.at[part], sems.at[k]))
            chunks[k].start()
        g = lax.broadcasted_iota(jnp.int32, (slopes, feats), 0)
        f = lax.broadcasted_iota(jnp.int32, (slopes, feats), 1)
        w[:slopes, :] = jnp.where(f == g * stride, 1.0, 0.0).astype(BF16)
        small[0].wait()
        w[slopes:, :] = b_ref[...].astype(BF16)
        small[1].wait()
        fill_table(table, [u_ref[c] for c in range(chains)])
        small[2].wait()
        for k in range(CHUNKS):
            chunks[k].wait()
            for t in range(k * size // TILE, (k + 1) * size // TILE):
                cols = slice(t * TILE, (t + 1) * TILE)
                both = lax.dot_general(w[...], kept[cols, :], NT, preferred_element_type=F32)
                slope_ref[:, cols] = both[:slopes, :].astype(BF16)
                linear[:, cols] = both[slopes:, :]
        all_terms(table, slope_ref, ids_ref, part_ref, chains, owned)
        part_ref[...] = SCALE * (part_ref[...] + linear[...])

    return pl.pallas_call(
        kernel,
        in_specs=[pl.BlockSpec(memory_space=pl.ANY)] * 4,
        out_specs=[whole(), whole()],
        out_shape=[
            jax.ShapeDtypeStruct((slopes, rows), BF16),
            jax.ShapeDtypeStruct((chains, rows), F32),
        ],
        scratch_shapes=[
            pltpu.VMEM((rows, feats), BF16),
            pltpu.VMEM((slopes + chains, feats), BF16),
            pltpu.VMEM((chains * owned, 2 * slopes), BF16),
            pltpu.VMEM((chains, rows), F32),
            pltpu.VMEM(ids.shape, jnp.int32),
            pltpu.VMEM(beta.shape, F32),
            pltpu.VMEM(pools.shape, F32),
            pltpu.SemaphoreType.DMA((3,)),
            pltpu.SemaphoreType.DMA((CHUNKS,)),
        ],
        compiler_params=params(),
        name="first_logits",
    )(in_hbm(design), in_hbm(ids), in_hbm(beta), in_hbm(pools))


def population_gradient(resid, design):
    planes = design.shape[1] // LANES

    def kernel(resid_ref, design_ref, out_ref):
        total = SCALE * lax.dot_general(
            resid_ref[...], design_ref[...], NN, preferred_element_type=F32
        )
        for k in range(planes):
            out_ref[k] = total[:, k * LANES : (k + 1) * LANES]

    return pl.pallas_call(
        kernel,
        in_specs=[whole(), whole()],
        out_specs=whole(),
        out_shape=jax.ShapeDtypeStruct((planes, resid.shape[0], LANES), F32),
        compiler_params=params(),
        name="population_gradient",
    )(resid, in_vmem(design))


def stacked_split(x, pieces):
    parts = []
    for _ in range(pieces):
        part = x.astype(BF16)
        parts.append(part)
        x = x - part.astype(F32)
    return jnp.concatenate(parts, axis=0)


def quad(x, j, pairs):
    return jnp.concatenate([x[k] for k in (2 * j, 2 * j + pairs, 2 * j + 1, 2 * j + 1 + pairs)], axis=1)


def region_onehot(index_ref, regions):
    shape = (regions, index_ref.shape[1])
    return jnp.where(lax.broadcasted_iota(jnp.int32, shape, 0) == index_ref[...], 1.0, 0.0)


def chosen_regions(onehot, v):
    chains, _, slopes = v.shape
    pairs = chains // 2
    table = jnp.concatenate([onehot.T.astype(BF16)] * 3, axis=1)
    found = [None] * chains
    for j in range(pairs // 2):
        got = lax.dot_general(
            table, stacked_split(quad(v, j, pairs), 3), NN, preferred_element_type=F32
        )
        for k, c in enumerate((2 * j, 2 * j + pairs, 2 * j + 1, 2 * j + 1 + pairs)):
            found[c] = got[:, k * slopes : (k + 1) * slopes]
    return found


def region_sums(onehot, x, pieces, store):
    pairs = len(x) // 2
    width = 2 * x[0].shape[1]
    table = jnp.concatenate([onehot.astype(BF16)] * pieces, axis=1)
    for j in range(pairs // 2):
        got = lax.dot_general(
            table, stacked_split(quad(x, j, pairs), pieces), NN, preferred_element_type=F32
        )
        store(2 * j, got[:, :width])
        store(2 * j + 1, got[:, width:])


def smem():
    return pl.BlockSpec(memory_space=pltpu.SMEM)


def prior(index, step, pools, regions, momentum, design):
    chains, owned, slopes = pools.shape
    n_regions = regions.shape[1]
    pairs = chains // 2

    def kernel(index_ref, step_ref, pools_ref, regions_ref, mom_ref, design_hbm, base_ref, sums_ref, kept, sems):
        size = design_hbm.shape[0] // COPIES
        copies = []
        for k in range(COPIES):
            part = pl.ds(k * size, size)
            copies.append(pltpu.make_async_copy(design_hbm.at[part], kept.at[part], sems.at[k]))
            copies[k].start()
        onehot = region_onehot(index_ref, n_regions)
        chosen = chosen_regions(onehot, regions_ref[...])
        dev = [PREC * (pools_ref[c] - chosen[c]) for c in range(chains)]
        for c in range(chains):
            base_ref[c] = mom_ref[c] - (0.5 * step_ref[c]) * dev[c]

        def store(k, value):
            sums_ref[k] = SCALE * value

        region_sums(onehot, dev, 3, store)
        count = jnp.sum(onehot, axis=1, keepdims=True)
        sums_ref[pairs] = SCALE * jnp.broadcast_to(count, (n_regions, 2 * slopes))
        for copy in copies:
            copy.wait()

    return pl.pallas_call(
        kernel,
        in_specs=[whole(), smem(), whole(), whole(), whole(), pl.BlockSpec(memory_space=pl.ANY)],
        out_specs=[whole()] * 3,
        out_shape=[
            jax.ShapeDtypeStruct(pools.shape, F32),
            jax.ShapeDtypeStruct((pairs + 1, n_regions, 2 * slopes), F32),
            pltpu.VMEM(design.shape, BF16),
        ],
        scratch_shapes=[pltpu.SemaphoreType.DMA((COPIES,))],
        compiler_params=params(),
        name="prior",
    )(index, step, pools, regions, momentum, in_hbm(design))


def pool_step(resid, slope, ids, index, step, base, mom_base, n_regions):
    chains, owned, slopes = base.shape
    rows = resid.shape[1]
    pairs = chains // 2

    def kernel(resid_ref, slope_ref, ids_ref, index_ref, step_ref, base_ref, mb_ref, next_ref, half_ref, term_ref, sums_ref, table, total):
        lik = all_sums(total, resid_ref, slope_ref, ids_ref, chains, owned)
        way, ahead = [], []
        for c in range(chains):
            half = mb_ref[c] + (0.5 * step_ref[c]) * lik[c]
            half_ref[c] = half
            way.append(step_ref[c] * half)
            ahead.append(base_ref[c] + way[c])
            next_ref[c] = ahead[c]
        fill_table(table, ahead)
        all_terms(table, slope_ref, ids_ref, term_ref, chains, owned)

        def store(k, value):
            sums_ref[k] = SCALE * value

        region_sums(region_onehot(index_ref, n_regions), way, 2, store)

    return pl.pallas_call(
        kernel,
        in_specs=[whole()] * 4 + [smem()] + [whole()] * 2,
        out_specs=[whole()] * 4,
        out_shape=[
            jax.ShapeDtypeStruct(base.shape, F32),
            jax.ShapeDtypeStruct(base.shape, F32),
            jax.ShapeDtypeStruct((chains, rows), F32),
            jax.ShapeDtypeStruct((pairs, n_regions, 2 * slopes), F32),
        ],
        scratch_shapes=[
            pltpu.VMEM((chains * owned, 2 * slopes), BF16),
            pltpu.VMEM((chains * owned, slopes), F32),
        ],
        compiler_params=params(),
        name="pool_step",
    )(resid, slope, ids, index, step, base, mom_base)


def finish(index, step, sums, regions, momentum, pool_part, gb, beta_next, beta_half, total_feats):
    chains, owned, slopes = pool_part.shape
    n_regions = regions.shape[1]
    pairs = chains // 2
    planes, _, lanes = gb.shape

    def kernel(index_ref, step_ref, column_ref, sums_ref, v_ref, m_ref, part_ref, gb_ref, b_ref, bh_ref, *rest):
        outs, (beta_ref, next_ref, mom_ref, pool_ref, sems) = rest[:4], rest[4:]
        copies = [
            pltpu.make_async_copy(made, out, sems.at[k])
            for k, (made, out) in enumerate(zip((beta_ref, next_ref, mom_ref, pool_ref), outs))
        ]
        h = 0.5 * column_ref[...]
        for k in range(planes):
            cols = slice(k * lanes, (k + 1) * lanes)
            grad = (1.0 / SCALE) * gb_ref[k] - total_feats * b_ref[:, cols]
            beta_ref[:, cols] = bh_ref[:, cols] + h * grad
        copies[0].start()

        def part(k, c):
            side = slice((c // pairs) * slopes, (c // pairs + 1) * slopes)
            return (1.0 / SCALE) * sums_ref[k + c % pairs][:, side]

        count = (1.0 / SCALE) * sums_ref[pairs][:, :slopes]
        for c in range(chains):
            v, h = v_ref[c], 0.5 * step_ref[c]
            dev = part(0, c)
            half = m_ref[c] + h * (dev - PREC * v)
            ahead = v + step_ref[c] * half
            next_ref[c] = ahead
            gain = dev + PREC * (part(pairs + 1, c) - count * (ahead - v)) - PREC * ahead
            mom_ref[c] = half + h * gain
        copies[1].start()
        copies[2].start()
        chosen = chosen_regions(region_onehot(index_ref, n_regions), next_ref[...])
        for c in range(chains):
            pool_ref[c] = part_ref[c] + (0.5 * step_ref[c]) * (PREC * chosen[c])
        copies[3].start()
        for copy in copies:
            copy.wait()

    made = [beta_next.shape, regions.shape, regions.shape, pool_part.shape]
    return pl.pallas_call(
        kernel,
        in_specs=[whole(), smem()] + [whole()] * 8,
        out_specs=[pl.BlockSpec(memory_space=pl.ANY)] * 4,
        out_shape=[pltpu.HBM(shape, F32) for shape in made],
        scratch_shapes=[pltpu.VMEM(shape, F32) for shape in made] + [pltpu.SemaphoreType.DMA((4,))],
        compiler_params=params(),
        name="finish",
    )(index, step, step[:, None], sums, regions, momentum, pool_part, gb, beta_next, beta_half)


def pool_likelihood(resid, slope, ids, step, half, pools_next):
    chains, owned, slopes = half.shape

    def kernel(resid_ref, slope_ref, ids_ref, step_ref, half_ref, u_ref, out_ref, total):
        lik = all_sums(total, resid_ref, slope_ref, ids_ref, chains, owned)
        for c in range(chains):
            out_ref[c] = half_ref[c] + (0.5 * step_ref[c]) * (lik[c] - PREC * u_ref[c])

    return pl.pallas_call(
        kernel,
        in_specs=[whole()] * 3 + [smem(), whole(), whole()],
        out_specs=whole(),
        out_shape=jax.ShapeDtypeStruct(half.shape, F32),
        scratch_shapes=[pltpu.VMEM((chains * owned, slopes), F32)],
        compiler_params=params(),
        name="pool_likelihood",
    )(resid, slope, ids, step, half, pools_next)


def next_logits(design, coef, term):
    rows = design.shape[0]

    def kernel(design_ref, coef_ref, term_ref, out_ref):
        coef16 = coef_ref[...].astype(BF16)
        for t in range(rows // TILE):
            cols = slice(t * TILE, (t + 1) * TILE)
            linear = lax.dot_general(coef16, design_ref[cols, :], NT, preferred_element_type=F32)
            out_ref[:, cols] = SCALE * (term_ref[:, cols] + linear)

    return pl.pallas_call(
        kernel,
        in_specs=[whole(), whole(), whole()],
        out_specs=whole(),
        out_shape=jax.ShapeDtypeStruct(term.shape, F32),
        compiler_params=params(),
        name="next_logits",
    )(in_vmem(design), coef, term)


def ahead_by(k, size, stride, group):
    perm = []
    for i in range(size):
        digit = (i // stride) % group
        perm.append((i, i + ((digit + k) % group - digit) * stride))
    return perm


def total_over(x, axis):
    size = lax.axis_size(axis)
    stride = 1
    while stride < size:
        group = min(4, size // stride)
        own = lax.optimization_barrier(x.astype(jnp.float16))
        parts = [own] + [
            lax.ppermute(own, axis, ahead_by(k, size, stride, group)) for k in range(1, group)
        ]
        parts = [p.astype(F32) for p in parts]
        x = parts[0] + parts[1] if group == 2 else (parts[0] + parts[2]) + (parts[1] + parts[3])
        stride *= group
    return x


def own_block(x, axis):
    size = lax.axis_size(axis)
    me = lax.axis_index(axis)
    width = x.shape[1] // size
    x = lax.optimization_barrier(x.astype(jnp.float16))

    def block(k):
        return lax.dynamic_slice_in_dim(x, lax.rem(me + k, size) * width, width, 1)

    mine = block(0).astype(F32)
    for k in range(1, size):
        mine = mine + lax.ppermute(block(k), axis, ahead_by(k, size, 1, size)).astype(F32)
    return mine.astype(jnp.float16)


def all_shifts(x, axis):
    size = lax.axis_size(axis)
    x = lax.optimization_barrier(x)
    return [x] + [lax.ppermute(x, axis, ahead_by(k, size, 1, size)) for k in range(1, size)]


def in_order(parts, axis):
    size = lax.axis_size(axis)
    me = lax.axis_index(axis)
    width = parts[0].shape[1]
    found = jnp.zeros((parts[0].shape[0], size * width) + parts[0].shape[2:], parts[0].dtype)
    for k, part in enumerate(parts):
        at = lax.rem(me + size - k, size) * width
        found = lax.dynamic_update_slice_in_dim(found, part, at, 1)
    return found.astype(F32)


def total_and_blocks(gb, mine, axis):
    size = lax.axis_size(axis)
    if size > 4 or mine.shape[1] != gb.shape[1] or mine.shape[2] != gb.shape[2]:
        return total_over(gb, axis), in_order(all_shifts(mine, axis), axis)
    planes = gb.shape[0]
    parts = all_shifts(jnp.concatenate([gb.astype(jnp.float16), mine], axis=0), axis)
    g = [part[:planes].astype(F32) for part in parts]
    total = g[0] if size == 1 else g[0] + g[1] if size == 2 else (g[0] + g[2]) + (g[1] + g[3])
    return total, in_order([part[planes:] for part in parts], axis)


def flat(planes):
    return jnp.concatenate(list(planes), axis=1)


def residual(part, labels):
    logit = total_over(part, "feat") * (1.0 / SCALE)
    return (labels.astype(F32)[None, :] - jax.nn.sigmoid(logit)).astype(BF16)


def body(
    design,
    labels,
    pool_ids,
    pool_region_index,
    step_size,
    beta,
    pools,
    regions,
    beta_momentum,
    pool_momentum,
    region_momentum,
):
    rows, feats = design.shape
    chains, owned, slopes = pools.shape
    n_regions = regions.shape[1]
    total_feats = float(feats * lax.axis_size("feat"))
    half = 0.5 * step_size
    ids = pool_ids[None, :]
    index = pool_region_index[None, :]

    slope, part = first_logits(design, ids, beta, pools, feats // slopes)
    pools_at, part = lax.optimization_barrier((pools, part))
    mom_base, dev_sums, kept = prior(
        index, step_size, pools_at, regions, pool_momentum, design
    )

    resid = residual(part, labels)
    gb = population_gradient(resid, kept)
    resid, gb, mom_base, dev_sums = lax.optimization_barrier((resid, gb, mom_base, dev_sums))
    pools_next, pool_half, term, way_sums = pool_step(
        resid, slope, ids, index, step_size, pools, mom_base, n_regions
    )
    mine = own_block(jnp.concatenate([dev_sums, way_sums], axis=0), "loan")
    gb = flat(total_over(gb, "loan")) * (1.0 / SCALE) - total_feats * beta
    beta_half = beta_momentum + half[:, None] * gb
    beta_next = beta + step_size[:, None] * beta_half

    part = next_logits(design, beta_next, term)
    resid = residual(part, labels)
    gb = population_gradient(resid, design)
    resid, gb = lax.optimization_barrier((resid, gb))
    pool_part = pool_likelihood(resid, slope, ids, step_size, pool_half, pools_next)
    gb, sums = total_and_blocks(gb, mine, "loan")
    beta_out, regions_next, region_out, pool_out = finish(
        index, step_size, sums, regions, region_momentum, pool_part, gb, beta_next, beta_half, total_feats
    )
    return (beta_next, pools_next, regions_next, beta_out, pool_out, region_out)


def solution(mesh):
    in_specs = (
        P(("grp", "loan"), "feat"),
        P(("grp", "loan")),
        P(("grp", "loan")),
        P(("grp", "loan")),
        P("grp"),
        P("grp", "feat"),
        P("grp", "loan", "feat"),
        P("grp", None, "feat"),
        P("grp", "feat"),
        P("grp", "loan", "feat"),
        P("grp", None, "feat"),
    )
    out_specs = (
        P("grp", "feat"),
        P("grp", "loan", "feat"),
        P("grp", None, "feat"),
        P("grp", "feat"),
        P("grp", "loan", "feat"),
        P("grp", None, "feat"),
    )
    return jax.shard_map(body, mesh=mesh, in_specs=in_specs, out_specs=out_specs, check_vma=False)
```
